128 devices in a mesh: line: 8 (over x, core), cross: 16 (over z, y).
Axes of the slice: x: 4, y: 4, z: 4, core: 2. Of those that a mesh axis runs over, the one named last changes fastest.
Arguments:
- state: float32 [5, 512, 128, 256], P(None, 'line', 'cross'), may hold values from -6 to 6
- axial_speed: float32 [512, 128, 256], P('line', 'cross'), may hold values from -4 to 4
- sound_speed: float32 [512, 128, 256], P('line', 'cross'), may hold values from 1 to 3
- cross_speed: float32 [512, 128, 256], P('line', 'cross'), may hold values from -4 to 4
- donor_base: int32 [8, 16, 16, 256], P('line', 'cross'), may hold values from 0 to 128766, as said below
- donor_frac: float32 [8, 16, 3, 16, 256], P('line', 'cross'), may hold values from 0 to 1
- fringe_cell: int32 [8, 16, 16, 256], P('line', 'cross'), may hold values from 0 to 131071, as said below
- live_count: int32 [8, 16, 16], P('line', 'cross'), may hold values from 1 to 256, as said below
Outputs:
- updated_state: float32 [5, 512, 128, 256], P(None, 'line', 'cross')
The draws below stay inside these ranges and needn't reach their ends.
Inputs may be any that keep to these rules, and one draw needn't show every extreme that they name: donor_base[l, c, p, s] = i*8*256 + j*256 + k with i < 63, j < 7, k < 255: the stencil's lowest corner in block (l, p). `fringe_cell`: the values of one device's block (l, c) are all distinct flat cell indices of that block. The used slots to donor p are the first live_count[l, c, p]; every device has a donor with all 256 slots used.
All inputs are finite; a program needn't handle non-finite values.
Results may differ from the reference program's by a relative error of at most 0.0003.
Values sent between devices are 32-bit elements; how exact they have to be, the bound alone decides.
A program may use at most 256 MiB of HBM per device.

```python
import math
import jax
import jax.numpy as jnp
from jax import lax

NV = 5
CL = 64
CJ = 8
NK = 256
CAP = 256
NL = 512
NJ = 128
N_LINE = 8
N_CROSS = 16


def draw_donor_base(key, part):
    key = jax.random.fold_in(key, 11)
    keys = jax.random.split(key, 3)
    shape = (N_LINE, N_CROSS, N_CROSS, CAP)
    along_line = jax.random.randint(keys[0], shape, 0, CL - 1)
    along_cross = jax.random.randint(keys[1], shape, 0, CJ - 1)
    along_depth = jax.random.randint(keys[2], shape, 0, NK - 1)
    return (along_line * (CJ * NK) + along_cross * NK + along_depth).astype(jnp.int32)


def draw_fringe_cell(key, part):
    key = jax.random.fold_in(key, 12)
    device_keys = jax.random.split(key, N_LINE * N_CROSS)
    chosen = jax.vmap(lambda k: jax.random.permutation(k, CL * CJ * NK)[:N_CROSS * CAP])(device_keys)
    return chosen.reshape(N_LINE, N_CROSS, N_CROSS, CAP).astype(jnp.int32)


def draw_live_count(key, part):
    key = jax.random.fold_in(key, 13)
    keys = jax.random.split(key, 3)
    popular = jax.random.randint(keys[0], (N_LINE, 1, N_CROSS), 1, 5)
    spread = jax.random.randint(keys[1], (N_LINE, N_CROSS, N_CROSS), 0, CAP)
    counts = jnp.minimum(CAP, 1 + spread * popular // 4)
    fullest = jax.random.randint(keys[2], (N_LINE, N_CROSS, 1), 0, N_CROSS)
    columns = jnp.arange(N_CROSS, dtype=jnp.int32)[None, None, :]
    return jnp.where(columns == fullest, CAP, counts).astype(jnp.int32)


def levels(own_key, shape, cuts, least, largest):
    gain = 1.0
    for position, blocks in cuts:
        steps = jax.random.uniform(jax.random.fold_in(jax.random.fold_in(own_key, 6), position), (blocks,), jnp.float32, least / len(cuts), largest / len(cuts))
        gain = gain * jnp.repeat(jnp.exp(steps), shape[position] // blocks).reshape((-1,) + (1,) * (len(shape) - 1 - position))
    return gain


def gaussian(own_key, extent, scale, limit, pieces=(), kind=jnp.bfloat16):
    values = scale * jax.random.normal(own_key, extent, jnp.float32)
    if pieces:
        values = values * levels(own_key, extent, pieces, -0.22, 0.18)
    return jnp.clip(values, -limit, limit).astype(kind)


def setup_inputs(seed: int = 0) -> dict:
    streams_of = jax.random.split(jax.random.key(seed), 9)
    return {
        "state": gaussian(streams_of[0], (NV, NL, NJ, NK), 1.0, 6.0, ((1, 8), (2, 16)), jnp.float32),
        "axial_speed": gaussian(streams_of[1], (NL, NJ, NK), 1.0, 4.0, ((0, 8), (1, 16)), jnp.float32),
        "sound_speed": jnp.clip(jnp.exp(math.log(3.0) - 1.0986123 * jax.random.uniform(streams_of[2], (NL, NJ, NK), jnp.float32) ** levels(streams_of[2], (NL, NJ, NK), ((0, 8), (1, 16)), -0.2, 0.2)), 1.0, 3.0),
        "cross_speed": gaussian(streams_of[3], (NL, NJ, NK), 1.0, 4.0, ((0, 8), (1, 16)), jnp.float32),
        "donor_base": draw_donor_base(jax.random.fold_in(streams_of[8], 71), 0),
        "donor_frac": jnp.clip(1.0 * jax.random.uniform(streams_of[5], (N_LINE, N_CROSS, 3, N_CROSS, CAP), jnp.float32) ** levels(streams_of[5], (N_LINE, N_CROSS, 3, N_CROSS, CAP), ((0, 8), (1, 16)), -0.2, 0.2), 0.0, 1.0),
        "fringe_cell": draw_fringe_cell(jax.random.fold_in(streams_of[8], 71), 0),
        "live_count": draw_live_count(jax.random.fold_in(streams_of[8], 71), 0),
    }


step_size = 8.0
implicit_second = 32.0
implicit_fourth = 0.25
explicit_line = 1.0
explicit_cross = 0.03125


def wave_signs():
    return jnp.array([-1.0, 0.0, 0.0, 0.0, 1.0], jnp.float32).reshape(5, 1, 1, 1)


def corner_offsets(plane_stride, row_stride):
    corner = jnp.arange(8, dtype=jnp.int32)
    return (corner // 4) * plane_stride + ((corner // 2) % 2) * row_stride + corner % 2


def corner_weights(fractions):
    along_x = (1.0 - fractions[0], fractions[0])
    along_y = (1.0 - fractions[1], fractions[1])
    along_z = (1.0 - fractions[2], fractions[2])
    return jnp.stack([along_x[k // 4] * along_y[(k // 2) % 2] * along_z[k % 2] for k in range(8)], 0)


def blend_corners(fractions, gathered):
    weights = corner_weights(fractions)
    return jnp.sum(jnp.moveaxis(weights, 0, 1)[None] * gathered, axis=2)


def place_fringe(flat_state, cell_index, counts, values):
    current = jnp.take(flat_state, cell_index, axis=1)
    live_slots = jnp.arange(cell_index.shape[1], dtype=jnp.int32)[None, :] < counts[:, None]
    chosen = jnp.where(live_slots[None], values, current)
    return flat_state.at[:, cell_index.reshape(-1)].set(chosen.reshape(5, -1))


def build_channels(values, axial, sound, crossing):
    speeds = axial[None] + wave_signs() * sound[None]
    return jnp.concatenate([speeds * values, crossing[None] * values, values, axial[None], sound[None]], 0)


def explicit_terms(padded):
    extent_rows = padded.shape[1] - 4
    extent_cols = padded.shape[2] - 4

    def window(i, j):
        return padded[:, 2 + i:2 + i + extent_rows, 2 + j:2 + j + extent_cols, :]

    middle = window(0, 0)
    values = middle[10:15]
    fourth_line = window(-2, 0)[10:15] - 4.0 * window(-1, 0)[10:15] + 6.0 * values - 4.0 * window(1, 0)[10:15] + window(2, 0)[10:15]
    fourth_cross = window(0, -2)[10:15] - 4.0 * window(0, -1)[10:15] + 6.0 * values - 4.0 * window(0, 1)[10:15] + window(0, 2)[10:15]
    spread = jnp.abs(middle[15:16]) + middle[16:17]
    speeds = middle[15:16] + wave_signs() * middle[16:17]
    operator_scale = spread + 0.5 * jnp.abs(speeds)
    source = (-step_size * 0.5 * (window(1, 0)[0:5] - window(-1, 0)[0:5])
              - step_size * 0.5 * (window(0, 1)[5:10] - window(0, -1)[5:10])
              - step_size * spread * (explicit_line * fourth_line + explicit_cross * fourth_cross))
    return source, operator_scale


def line_coefficients(operator_scale):
    lower_two = step_size * implicit_fourth * operator_scale
    lower_one = -step_size * (implicit_second + 4.0 * implicit_fourth) * operator_scale
    centre = 1.0 + step_size * (2.0 * implicit_second + 6.0 * implicit_fourth) * operator_scale
    return lower_two, lower_one, centre


def forward_row(state_in, coefficient_row):
    prior_lead, prior_tail, prior_value, recent_lead, recent_tail, recent_value = state_in
    operator_scale, source = coefficient_row
    lower_two, lower_one, centre = line_coefficients(operator_scale)
    shifted_lower = lower_one - lower_two * prior_lead
    diagonal_term = centre - lower_two * prior_tail
    right_term = source - lower_two * prior_value
    diagonal_term = diagonal_term - shifted_lower * recent_lead
    upper_term = lower_one - shifted_lower * recent_tail
    right_term = right_term - shifted_lower * recent_value
    new_lead = upper_term / diagonal_term
    new_tail = lower_two / diagonal_term
    new_value = right_term / diagonal_term
    return (recent_lead, recent_tail, recent_value, new_lead, new_tail, new_value), (new_lead, new_tail, new_value)


def backward_row(state_in, factor_row):
    next_value, after_value = state_in
    lead_row, tail_row, value_row = factor_row
    solved = value_row - lead_row * next_value - tail_row * after_value
    return (solved, next_value), solved


def line_solve(operator_scale, source):
    zeros_row = jnp.zeros((5, source.shape[2]), jnp.float32)
    moved = tuple(jnp.moveaxis(x, 1, 0) for x in (operator_scale, source))
    _, factors = lax.scan(forward_row, (zeros_row,) * 6, moved)
    _, solved = lax.scan(backward_row, (zeros_row, zeros_row), factors, reverse=True)
    return jnp.moveaxis(solved, 0, 1)


def reference(state, axial_speed, sound_speed, cross_speed, donor_base, donor_frac, fringe_cell, live_count):
    cell_count = CL * CJ * NK
    blocks = state.reshape(5, N_LINE, CL, N_CROSS, CJ, NK).transpose(1, 3, 0, 2, 4, 5).reshape(N_LINE, N_CROSS, 5, cell_count)
    offsets = corner_offsets(CJ * NK, NK)

    def one_line(operands):
        line_blocks, line_base, line_frac = operands

        def one_receiver(receiver_base, receiver_frac):
            indices = receiver_base[:, None, :] + offsets[None, :, None]
            gathered = jax.vmap(lambda b, i: jnp.take(b, i, axis=1), in_axes=(0, 0), out_axes=1)(line_blocks, indices)
            return blend_corners(receiver_frac, gathered)

        return jax.vmap(one_receiver)(line_base, line_frac)

    donor_value = lax.map(one_line, (blocks, donor_base, donor_frac))
    placed = jax.vmap(jax.vmap(place_fringe))(blocks, fringe_cell, live_count, donor_value)
    fringe_state = placed.reshape(N_LINE, N_CROSS, 5, CL, CJ, NK).transpose(2, 0, 3, 1, 4, 5).reshape(5, N_LINE * CL, N_CROSS * CJ, NK)
    channels = build_channels(fringe_state, axial_speed, sound_speed, cross_speed)
    padded = jnp.pad(channels, ((0, 0), (2, 2), (2, 2), (0, 0)))
    source, operator_scale = explicit_terms(padded)
    delta = line_solve(operator_scale.reshape(5, N_LINE * CL, -1), source.reshape(5, N_LINE * CL, -1))
    return fringe_state + delta.reshape(fringe_state.shape)
```

```python
import functools

import jax
import jax.numpy as jnp
from jax import lax
from jax.experimental import pallas as pl
from jax.experimental.pallas import tpu as pltpu
from jax.sharding import PartitionSpec as P

MESH = pl.DeviceIdType.MESH
F32 = jnp.float32
BF16 = jnp.bfloat16
NV, CL, CJ, NK, CAP = 5, 64, 8, 256, 256
NLINE, NCROSS = 8, 16
SETS = (0, 1, 1, 1, 2)
SIGMA = (-1.0, 0.0, 1.0)
ONE, TWO, MID = -264.0, 2.0, 524.0
BIG = 60 * 1024 * 1024

VMEM_SPEC = pl.BlockSpec(memory_space=pltpu.VMEM)
SMEM_SPEC = pl.BlockSpec(memory_space=pltpu.SMEM)
ANY_SPEC = pl.BlockSpec(memory_space=pl.ANY)


def greet(peers):
    barrier = pltpu.get_barrier_semaphore()
    for peer in peers:
        pl.semaphore_signal(barrier, inc=1, device_id=peer, device_id_type=MESH)
    pl.semaphore_wait(barrier, len(peers))


def remote(src, dst, send, recv, device):
    copy = pltpu.make_async_remote_copy(
        src_ref=src, dst_ref=dst, send_sem=send, recv_sem=recv, device_id=device, device_id_type=MESH
    )
    copy.start()
    return copy


def around(axis):
    count = {"line": NLINE, "cross": NCROSS}[axis]
    me = lax.axis_index(axis)
    return me, [lax.rem(me + d, count) for d in range(1, count)]


def request_kernel(
    base, frac, axial, sound, crossing, inbox, line_in, cross_in, packed, line_out, cross_out, send, recv, own
):
    me, peers = around("cross")
    row = lax.axis_index("line")
    down, up = lax.rem(row + 1, NLINE), lax.rem(row + NLINE - 1, NLINE)
    right, left = lax.rem(me + 1, NCROSS), lax.rem(me + NCROSS - 1, NCROSS)
    for half in range(2):
        lanes = pl.ds(half * 128, 128)
        packed[:, half, :] = base[:, lanes].astype(F32)
        for q in range(3):
            packed[:, 2 * q + 2 + half, :] = frac[q, :, lanes]
    line_out[0] = axial[0]
    line_out[1] = sound[0]
    line_out[2] = axial[CL - 1]
    line_out[3] = sound[CL - 1]
    cross_out[0] = crossing[:, 0, :]
    cross_out[1] = crossing[:, CJ - 1, :]
    greet([(row, p) for p in peers] + [(down, me), (up, me)])
    copies = []
    for d, p in enumerate(peers):
        copies.append(remote(packed.at[p], inbox.at[me], send.at[d], recv.at[d], (row, p)))
    copies.append(remote(line_out.at[pl.ds(0, 2)], line_in.at[pl.ds(2, 2)], send.at[15], recv.at[15], (up, me)))
    copies.append(remote(line_out.at[pl.ds(2, 2)], line_in.at[pl.ds(0, 2)], send.at[16], recv.at[16], (down, me)))
    copies.append(remote(cross_out.at[0], cross_in.at[1], send.at[17], recv.at[17], (row, left)))
    copies.append(remote(cross_out.at[1], cross_in.at[0], send.at[18], recv.at[18], (row, right)))
    kept = pltpu.make_async_copy(packed.at[me], inbox.at[me], own)
    kept.start()
    for copy in copies:
        copy.wait()
    kept.wait()


def send_requests(base, frac, axial, sound, crossing):
    return pl.pallas_call(
        request_kernel,
        out_shape=(
            jax.ShapeDtypeStruct((NCROSS, 8, 128), F32),
            jax.ShapeDtypeStruct((4, CJ, NK), F32),
            jax.ShapeDtypeStruct((2, CL, NK), F32),
        ),
        in_specs=[VMEM_SPEC] * 5,
        out_specs=(VMEM_SPEC,) * 3,
        scratch_shapes=[
            pltpu.VMEM((NCROSS, 8, 128), F32),
            pltpu.VMEM((4, CJ, NK), F32),
            pltpu.VMEM((2, CL, NK), F32),
            pltpu.SemaphoreType.DMA((19,)),
            pltpu.SemaphoreType.DMA((19,)),
            pltpu.SemaphoreType.DMA,
        ],
        compiler_params=pltpu.CompilerParams(collective_id=0, has_side_effects=True),
        name="send_requests",
    )(base, frac, axial, sound, crossing)


def swap_kernel(axis, *refs):
    n = (len(refs) - 3) // 2
    sources, targets = refs[:n], refs[n : 2 * n]
    send, recv, own = refs[2 * n :]
    me, peers = around(axis)
    other = lax.axis_index("cross" if axis == "line" else "line")

    def place(p):
        return (p, other) if axis == "line" else (other, p)

    greet([place(p) for p in peers])
    copies = []
    for m in range(n):
        for d, p in enumerate(peers):
            copies.append(remote(sources[m].at[p], targets[m].at[me], send.at[m, d], recv.at[m, d], place(p)))
        kept = pltpu.make_async_copy(sources[m].at[me], targets[m].at[me], own.at[m])
        kept.start()
        copies.append(kept)
    for copy in copies:
        copy.wait()


def swap(axis, ident, name, *arrays):
    n = len(arrays)
    count = arrays[0].shape[0]
    return pl.pallas_call(
        functools.partial(swap_kernel, axis),
        out_shape=tuple(jax.ShapeDtypeStruct(a.shape, a.dtype) for a in arrays),
        in_specs=[VMEM_SPEC] * n,
        out_specs=(VMEM_SPEC,) * n,
        scratch_shapes=[
            pltpu.SemaphoreType.DMA((n, count - 1)),
            pltpu.SemaphoreType.DMA((n, count - 1)),
            pltpu.SemaphoreType.DMA((n,)),
        ],
        compiler_params=pltpu.CompilerParams(collective_id=ident, has_side_effects=True),
        name=name,
    )(*arrays)


def donor_kernel(request, state, out, left, right):
    @pl.when(pl.program_id(0) == 0)
    def _():
        for v in range(NV):
            flipped = state[v].T
            high = flipped.astype(BF16)
            low = (flipped - high.astype(F32)).astype(BF16)
            left[v, :, 0:512] = high
            left[v, :, 512:1024] = low
            left[v, :, 1024:1536] = high

    def row(q):
        return jnp.concatenate([request[0, 2 * q : 2 * q + 1, :], request[0, 2 * q + 1 : 2 * q + 2, :]], 1)

    base = row(0).astype(jnp.int32)
    fx, fy, fz = row(1), row(2), row(3)
    gx, gy, gz = 1.0 - fx, 1.0 - fy, 1.0 - fz
    first = lax.shift_right_logical(base, 8)
    depth = lax.bitwise_and(base, 255)
    away = lax.broadcasted_iota(jnp.int32, (512, 256), 0) - first
    weight = jnp.where(
        away == 0,
        gx * gy,
        jnp.where(away == 1, gx * fy, jnp.where(away == 8, fx * gy, jnp.where(away == 9, fx * fy, 0.0))),
    )
    high = weight.astype(BF16)
    low = (weight - high.astype(F32)).astype(BF16)
    right[0:512] = high
    right[512:1024] = high
    right[1024:1536] = low
    past = lax.broadcasted_iota(jnp.int32, (256, 256), 0) - depth
    along = jnp.where(past == 0, gz, jnp.where(past == 1, fz, 0.0))
    out[0] = jnp.zeros((8, 256), F32)
    for v in range(NV):
        mixed = jnp.dot(left[v], right[...], preferred_element_type=F32)
        out[0, v : v + 1, :] = jnp.sum(mixed * along, axis=0, keepdims=True)


def donor_values(requests, state):
    return pl.pallas_call(
        donor_kernel,
        grid=(NCROSS,),
        out_shape=jax.ShapeDtypeStruct((NCROSS, 8, CAP), F32),
        in_specs=[
            pl.BlockSpec((1, 8, 128), lambda p: (p, 0, 0)),
            pl.BlockSpec((NV, 512, NK), lambda p: (0, 0, 0)),
        ],
        out_specs=pl.BlockSpec((1, 8, CAP), lambda p: (p, 0, 0)),
        scratch_shapes=[pltpu.VMEM((NV, NK, 1536), BF16), pltpu.VMEM((1536, CAP), BF16)],
        compiler_params=pltpu.CompilerParams(vmem_limit_bytes=BIG),
        name="donor_values",
    )(requests, state)


def fringe_kernel(live, cell, value, state, out, head, tail, along, spread):
    step = pl.program_id(0)

    def live_rows(p):
        here = cell[p : p + 1, :]
        used = lax.broadcasted_iota(jnp.int32, (1, CAP), 1) < live[p]
        return jnp.where(used, lax.shift_right_logical(here, 8), -1), lax.bitwise_and(here, 255)

    @pl.when(step == 0)
    def _():
        for p in range(NCROSS):
            _, depth = live_rows(p)
            hit = lax.broadcasted_iota(jnp.int32, (NK, CAP), 0) == depth
            along[:, p * CAP : (p + 1) * CAP] = jnp.where(hit, 1.0, 0.0).astype(BF16)

    for p in range(NCROSS):
        lanes = slice(p * CAP, (p + 1) * CAP)
        cell_row, _ = live_rows(p)
        hit = lax.broadcasted_iota(jnp.int32, (64, CAP), 0) + step * 64 == cell_row
        picked = jnp.where(hit, 1.0, 0.0).astype(BF16)
        for v in range(NV):
            values = value[p, v : v + 1, :]
            high = values.astype(BF16)
            low = (values - high.astype(F32)).astype(BF16)
            spread[v * 64 : v * 64 + 64, lanes] = picked * high
            spread[(NV + v) * 64 : (NV + v) * 64 + 64, lanes] = picked * low
        spread[2 * NV * 64 : (2 * NV + 1) * 64, lanes] = picked
    placed = lax.dot_general(
        spread[...], along[...], (((1,), (1,)), ((), ())), preferred_element_type=F32
    )
    taken = placed[2 * NV * 64 :] > 0.5
    for v in range(NV):
        fresh = placed[v * 64 : v * 64 + 64] + placed[(NV + v) * 64 : (NV + v) * 64 + 64]
        now = jnp.where(taken, fresh, state[v].reshape(64, NK)).reshape(8, CJ, NK)
        out[v] = now
        for j in range(2):
            head[v, j] = now[:, j, :]
            tail[v, j] = now[:, CJ - 2 + j, :]


def fringe_state(live, cell, value, state):
    edge = jax.ShapeDtypeStruct((NV, 2, CL, NK), F32)
    edge_spec = pl.BlockSpec((NV, 2, 8, NK), lambda t: (0, 0, t, 0))
    return pl.pallas_call(
        fringe_kernel,
        grid=(CL // 8,),
        out_shape=(jax.ShapeDtypeStruct((NV, CL, CJ, NK), F32), edge, edge),
        in_specs=[
            SMEM_SPEC,
            pl.BlockSpec((NCROSS, CAP), lambda t: (0, 0)),
            pl.BlockSpec((NCROSS, 8, CAP), lambda t: (0, 0, 0)),
            pl.BlockSpec((NV, 8, CJ, NK), lambda t: (0, t, 0, 0)),
        ],
        out_specs=(pl.BlockSpec((NV, 8, CJ, NK), lambda t: (0, t, 0, 0)), edge_spec, edge_spec),
        scratch_shapes=[pltpu.VMEM((NK, NCROSS * CAP), BF16), pltpu.VMEM((11 * 64, NCROSS * CAP), BF16)],
        compiler_params=pltpu.CompilerParams(vmem_limit_bytes=BIG),
        name="fringe_state",
    )(live, cell, value, state)


def halo_kernel(state, head, tail, above, below, before, after, send, recv):
    me, row = lax.axis_index("cross"), lax.axis_index("line")
    down, up = lax.rem(row + 1, NLINE), lax.rem(row + NLINE - 1, NLINE)
    right, left = lax.rem(me + 1, NCROSS), lax.rem(me + NCROSS - 1, NCROSS)
    greet([(row, left), (row, right), (up, me), (down, me)])
    copies = [
        remote(head, after, send.at[0], recv.at[0], (row, left)),
        remote(tail, before, send.at[1], recv.at[1], (row, right)),
        remote(state.at[:, pl.ds(0, 2)], below, send.at[2], recv.at[2], (up, me)),
        remote(state.at[:, pl.ds(CL - 2, 2)], above, send.at[3], recv.at[3], (down, me)),
    ]
    for copy in copies:
        copy.wait()


def swap_halos(state, head, tail):
    ends = jax.ShapeDtypeStruct((NV, 2, CJ, NK), F32)
    edge = jax.ShapeDtypeStruct((NV, 2, CL, NK), F32)
    return pl.pallas_call(
        halo_kernel,
        out_shape=(ends, ends, edge, edge),
        in_specs=[ANY_SPEC] * 3,
        out_specs=(ANY_SPEC,) * 4,
        scratch_shapes=[pltpu.SemaphoreType.DMA((4,)), pltpu.SemaphoreType.DMA((4,))],
        compiler_params=pltpu.CompilerParams(collective_id=1, has_side_effects=True),
        name="swap_halos",
    )(state, head, tail)


def factor_kernel(axial, sound, lead, tail, first, second, inverse, corners):
    zero = sound[0] * 0.0
    corners[...] = jnp.zeros(corners.shape, F32)

    def body(i, carried):
        speed, wave = axial[i], sound[i]
        rho = jnp.abs(speed) + wave
        after = []
        for s in range(3):
            e1, p1, q1, q2, a1, a2, b1, b2, aa, ab, bb = carried[s]
            scale = rho + 0.5 * jnp.abs(speed + SIGMA[s] * wave)
            r = 1.0 / scale
            d = (MID + r) - TWO * q2 - e1 * p1
            inv = 1.0 / d
            e = ONE - TWO * p1
            p = e * inv
            q = TWO * inv
            start = jnp.where(i == 0, 1.0, 0.0)
            following = jnp.where(i == 1, 1.0, 0.0)
            a = start - p1 * a1 - q2 * a2
            b = following - p1 * b1 - q2 * b2
            ai, bi = a * inv, b * inv
            lead[s, i], tail[s, i], first[s, i], second[s, i], inverse[s, i] = p, q, a, b, r
            after.append((e, p, q, q1, a, a1, b, b1, aa + ai * a, ab + ai * b, bb + bi * b))
        return tuple(after)

    done = lax.fori_loop(0, CL, body, (((zero,) * 11),) * 3, unroll=4)
    for s in range(3):
        _, _, q1, q2, a1, a2, b1, b2, aa, ab, bb = done[s]
        inv1, inv2, p2 = 0.5 * q1, 0.5 * q2, lead[s, CL - 2]
        entries = (
            aa,
            ab,
            bb,
            a2 * inv2 - a1 * p2 * inv1,
            a1 * inv1,
            b2 * inv2 - b1 * p2 * inv1,
            b1 * inv1,
            inv2 + p2 * p2 * inv1,
            -p2 * inv1,
            inv1,
        )
        for m, entry in enumerate(entries):
            corners[:, 3 * m + s, :] = entry


def factor(axial, sound):
    full = jax.ShapeDtypeStruct((3, CL, CJ, NK), F32)
    full_spec = pl.BlockSpec((3, CL, CJ, 128), lambda h: (0, 0, 0, h))
    speed_spec = pl.BlockSpec((CL, CJ, 128), lambda h: (0, 0, h))
    return pl.pallas_call(
        factor_kernel,
        grid=(2,),
        out_shape=(full,) * 5 + (jax.ShapeDtypeStruct((CJ, 32, NK), F32),),
        in_specs=[speed_spec] * 2,
        out_specs=(full_spec,) * 5 + (pl.BlockSpec((CJ, 32, 128), lambda h: (0, 0, h)),),
        compiler_params=pltpu.CompilerParams(vmem_limit_bytes=BIG),
        name="factor",
    )(axial, sound)


def forward_kernel(
    where, state, above, below, before, after, axial, sound, crossing, line_halo, cross_halo,
    lead, tail, first, second, inverse, out, ends, full, speeds, waves,
):
    line, cross = where[0], where[1]
    ends[...] = jnp.zeros(ends.shape, F32)

    def inside(flag, value):
        return jnp.where(flag, value, 0.0)

    for v in range(NV):
        full[v, pl.ds(2, CL)] = state[v]
        full[v, pl.ds(0, 2)] = inside(line > 0, above[v])
        full[v, pl.ds(CL + 2, 2)] = inside(line < NLINE - 1, below[v])
    speeds[pl.ds(1, CL)] = axial[...]
    waves[pl.ds(1, CL)] = sound[...]
    speeds[0], waves[0] = line_halo[0], line_halo[1]
    speeds[CL + 1], waves[CL + 1] = line_halo[2], line_halo[3]
    column = lax.broadcasted_iota(jnp.int32, (CJ, 128), 0)
    zero = sound[0] * 0.0
    has_left, has_right = cross > 0, cross < NCROSS - 1

    def body(i, carried):
        speed, wave, crosses = axial[i], sound[i], crossing[i]
        rho = jnp.abs(speed) + wave
        speed_up, wave_up = speeds[i], waves[i]
        speed_down, wave_down = speeds[i + 2], waves[i + 2]
        row = pl.ds(i, 1)
        cross_left = jnp.where(column == 0, cross_halo[0, row, :], pltpu.roll(crosses, 1, 0))
        cross_right = jnp.where(column == CJ - 1, cross_halo[1, row, :], pltpu.roll(crosses, CJ - 1, 0))
        following = []
        for v in range(NV):
            s = SETS[v]
            y1, y2, low, high = carried[v]
            q = full[v, i + 2]
            up, down = full[v, i + 1], full[v, i + 3]
            fourth = full[v, i] + full[v, i + 4] - 4.0 * (up + down) + 6.0 * q
            l2 = inside(has_left, before[v, 0, row, :])
            l1 = inside(has_left, before[v, 1, row, :])
            r1 = inside(has_right, after[v, 0, row, :])
            r2 = inside(has_right, after[v, 1, row, :])
            left1 = jnp.where(column == 0, l1, pltpu.roll(q, 1, 0))
            left2 = jnp.where(column == 0, l2, jnp.where(column == 1, l1, pltpu.roll(q, 2, 0)))
            right1 = jnp.where(column == CJ - 1, r1, pltpu.roll(q, CJ - 1, 0))
            right2 = jnp.where(column == CJ - 1, r2, jnp.where(column == CJ - 2, r1, pltpu.roll(q, CJ - 2, 0)))
            fourth_cross = left2 + right2 - 4.0 * (left1 + right1) + 6.0 * q
            lam_up = speed_up + SIGMA[s] * wave_up
            lam_down = speed_down + SIGMA[s] * wave_down
            source = (
                -4.0 * (lam_down * down - lam_up * up)
                - 4.0 * (cross_right * right1 - cross_left * left1)
                - 8.0 * rho * (fourth + 0.03125 * fourth_cross)
            )
            p1 = lead[s, jnp.maximum(i - 1, 0)]
            q2 = tail[s, jnp.maximum(i - 2, 0)]
            y = source * inverse[s, i] - p1 * y1 - q2 * y2
            out[v, i] = y
            t = y * (0.5 * tail[s, i])
            following.append((y, y1, low + first[s, i] * t, high + second[s, i] * t))
        return tuple(following)

    done = lax.fori_loop(0, CL, body, (((zero,) * 4),) * NV, unroll=2)
    for v in range(NV):
        s = SETS[v]
        y1, y2, low, high = done[v]
        last = 0.5 * tail[s, CL - 1] * y1
        ends[:, v, :] = low
        ends[:, 8 + v, :] = high
        ends[:, 16 + v, :] = 0.5 * tail[s, CL - 2] * y2 - lead[s, CL - 2] * last
        ends[:, 24 + v, :] = last


def forward(place, state, halos, axial, sound, crossing, line_halo, cross_halo, factors):
    def lanes(*sizes):
        zeros = (0,) * len(sizes)
        return pl.BlockSpec(sizes + (128,), lambda h: zeros + (h,))

    return pl.pallas_call(
        forward_kernel,
        grid=(2,),
        out_shape=(
            jax.ShapeDtypeStruct((NV, CL, CJ, NK), F32),
            jax.ShapeDtypeStruct((CJ, 32, NK), F32),
        ),
        in_specs=[SMEM_SPEC, lanes(NV, CL, CJ), lanes(NV, 2, CJ), lanes(NV, 2, CJ), lanes(NV, 2, CL), lanes(NV, 2, CL)]
        + [lanes(CL, CJ)] * 3
        + [lanes(4, CJ), lanes(2, CL)]
        + [lanes(3, CL, CJ)] * 5,
        out_specs=(lanes(NV, CL, CJ), lanes(CJ, 32)),
        scratch_shapes=[
            pltpu.VMEM((NV, CL + 4, CJ, 128), F32),
            pltpu.VMEM((CL + 2, CJ, 128), F32),
            pltpu.VMEM((CL + 2, CJ, 128), F32),
        ],
        compiler_params=pltpu.CompilerParams(vmem_limit_bytes=BIG),
        name="forward",
    )(place, state, *halos, axial, sound, crossing, line_halo, cross_halo, *factors)


def times(m, n):
    a, b, c, d = m
    e, f, g, h = n
    return (a * e + b * g, a * f + b * h, c * e + d * g, c * f + d * h)


def apply(m, x):
    return (m[0] * x[0] + m[1] * x[1], m[2] * x[0] + m[3] * x[1])


def right_upper(m):
    return (TWO * m[0], ONE * m[0] + TWO * m[1], TWO * m[2], ONE * m[2] + TWO * m[3])


def right_lower(m):
    return (TWO * m[0] + ONE * m[1], TWO * m[1], TWO * m[2] + ONE * m[3], TWO * m[3])


def plus(m, n):
    return tuple(a + b for a, b in zip(m, n))


def minus(m, n):
    return tuple(a - b for a, b in zip(m, n))


def interface_kernel(ends, corners, out):
    variable = lax.broadcasted_iota(jnp.int32, (8, NK), 0)

    def corner(l, m):
        rows = [corners[l, 3 * m + s : 3 * m + s + 1, :] for s in range(3)]
        return jnp.where(variable == 0, rows[0], jnp.where(variable == 4, rows[2], rows[1]))

    steps = []
    p = m = None
    for l in range(NLINE):
        c = [corner(l, k) for k in range(10)]
        heads = (c[0], c[1], c[1], c[2])
        cross = (c[3], c[4], c[5], c[6])
        back = (c[3], c[5], c[4], c[6])
        tails = (c[7], c[8], c[8], c[9])
        ya = (ends[l, 0:8, :], ends[l, 8:16, :])
        yb = (ends[l, 16:24, :], ends[l, 24:32, :])
        if l == 0:
            inner, reach = ya, right_lower(cross)
            p, m = yb, right_lower(tails)
        else:
            heads_u, back_u = right_upper(heads), right_upper(back)
            t = times(heads_u, m)
            g = (1.0 - t[0], -t[1], -t[2], 1.0 - t[3])
            scale = 1.0 / (g[0] * g[3] - g[1] * g[2])
            g = (g[3] * scale, -g[1] * scale, -g[2] * scale, g[0] * scale)
            inner = apply(g, minus(ya, apply(heads_u, p)))
            reach = right_lower(times(g, cross))
            back_um = times(back_u, m)
            p = plus(minus(yb, apply(back_u, p)), apply(back_um, inner))
            m = plus(right_lower(tails), times(back_um, reach))
        steps.append((inner, reach, p, m))
    a = None
    for l in reversed(range(NLINE)):
        inner, reach, _, _ = steps[l]
        zero = ends[0, 0:8, :] * 0.0
        if l == NLINE - 1:
            beta = (zero, zero)
            a = inner
        else:
            beta = (TWO * a[0], ONE * a[0] + TWO * a[1])
            a = minus(inner, apply(reach, a))
        if l == 0:
            alpha = (zero, zero)
        else:
            _, _, p, m = steps[l - 1]
            b = minus(p, apply(m, a))
            alpha = (TWO * b[0] + ONE * b[1], TWO * b[1])
        out[l, 0:8, :] = alpha[0]
        out[l, 8:16, :] = alpha[1]
        out[l, 16:24, :] = beta[0]
        out[l, 24:32, :] = beta[1]


def interface(ends, corners):
    return pl.pallas_call(
        interface_kernel,
        out_shape=jax.ShapeDtypeStruct((NLINE, 32, NK), F32),
        in_specs=[VMEM_SPEC] * 2,
        out_specs=VMEM_SPEC,
        name="interface",
    )(ends, corners)


def backward_kernel(forces, eliminated, state, lead, tail, first, second, out):
    def forced(v, i):
        s = SETS[v]
        alpha0, alpha1 = forces[:, v, :], forces[:, 8 + v, :]
        return eliminated[v, i] - first[s, i] * alpha0 - second[s, i] * alpha1

    start = []
    for v in range(NV):
        s = SETS[v]
        beta0, beta1 = forces[:, 16 + v, :], forces[:, 24 + v, :]
        p2 = lead[s, CL - 2]
        last = (forced(v, CL - 1) - beta1 + p2 * beta0) * (0.5 * tail[s, CL - 1])
        prior = (forced(v, CL - 2) - beta0) * (0.5 * tail[s, CL - 2]) - p2 * last
        out[v, CL - 1] = state[v, CL - 1] + last
        out[v, CL - 2] = state[v, CL - 2] + prior
        start.append((prior, last))

    def body(t, carried):
        i = CL - 3 - t
        following = []
        for v in range(NV):
            s = SETS[v]
            x1, x2 = carried[v]
            q = tail[s, i]
            x = (0.5 * forced(v, i) - x2) * q - lead[s, i] * x1
            out[v, i] = state[v, i] + x
            following.append((x, x1))
        return tuple(following)

    lax.fori_loop(0, CL - 2, body, tuple(start), unroll=2)


def backward(forces, eliminated, state, lead, tail, first, second):
    def lanes(*sizes):
        zeros = (0,) * len(sizes)
        return pl.BlockSpec(sizes + (128,), lambda h: zeros + (h,))

    return pl.pallas_call(
        backward_kernel,
        grid=(2,),
        out_shape=jax.ShapeDtypeStruct((NV, CL, CJ, NK), F32),
        in_specs=[lanes(CJ, 32), lanes(NV, CL, CJ), lanes(NV, CL, CJ)] + [lanes(3, CL, CJ)] * 4,
        out_specs=lanes(NV, CL, CJ),
        compiler_params=pltpu.CompilerParams(vmem_limit_bytes=BIG),
        name="backward",
    )(forces, eliminated, state, lead, tail, first, second)


def on_device(
    state, axial_speed, sound_speed, cross_speed, donor_base, donor_frac, fringe_cell, live_count
):
    place = jnp.stack([lax.axis_index("line"), lax.axis_index("cross")]).astype(jnp.int32)
    requests, line_halo, cross_halo = send_requests(
        donor_base.reshape(NCROSS, CAP),
        donor_frac.reshape(3, NCROSS, CAP),
        axial_speed,
        sound_speed,
        cross_speed,
    )
    values = donor_values(requests, state.reshape(NV, CL * CJ, NK))
    (values,) = swap("cross", 2, "return_values", values)
    fringe, head, tail = fringe_state(
        live_count.reshape(NCROSS), fringe_cell.reshape(NCROSS, CAP), values, state
    )
    above, below, before, after = swap_halos(fringe, head, tail)
    *factors, corners = factor(axial_speed, sound_speed)
    eliminated, ends = forward(
        place,
        fringe,
        (above, below, before, after),
        axial_speed,
        sound_speed,
        cross_speed,
        line_halo,
        cross_halo,
        factors,
    )
    ends, corners = swap("line", 3, "share_ends", ends, corners)
    (forces,) = swap("line", 4, "share_forces", interface(ends, corners))
    return backward(forces, eliminated, fringe, *factors[:4])


def solution(mesh):
    in_specs = (
        P(None, "line", "cross", None),
        P("line", "cross", None),
        P("line", "cross", None),
        P("line", "cross", None),
        P("line", "cross", None, None),
        P("line", "cross", None, None, None),
        P("line", "cross", None, None),
        P("line", "cross", None),
    )
    out_specs = P(None, "line", "cross", None)
    return jax.shard_map(
        on_device, mesh=mesh, in_specs=in_specs, out_specs=out_specs, check_vma=False
    )
```

```python
import functools

import jax
import jax.numpy as jnp
from jax import lax
from jax.experimental import pallas as pl
from jax.experimental.pallas import tpu as pltpu
from jax.sharding import PartitionSpec as P

MESH = pl.DeviceIdType.MESH
F32 = jnp.float32
BF16 = jnp.bfloat16
NV, CL, CJ, NK, CAP = 5, 64, 8, 256, 256
NLINE, NCROSS = 8, 16
SETS = (0, 1, 1, 1, 2)
SIGMA = (-1.0, 0.0, 1.0)
ONE, TWO, MID = -264.0, 2.0, 524.0
FRONT = 40 * 1024 * 1024
MIDDLE = 40 * 1024 * 1024
BIG = 40 * 1024 * 1024

VMEM_SPEC = pl.BlockSpec(memory_space=pltpu.VMEM)
SMEM_SPEC = pl.BlockSpec(memory_space=pltpu.SMEM)
ANY_SPEC = pl.BlockSpec(memory_space=pl.ANY)


def greet(peers):
    barrier = pltpu.get_barrier_semaphore()
    for peer in peers:
        pl.semaphore_signal(barrier, inc=1, device_id=peer, device_id_type=MESH)
    pl.semaphore_wait(barrier, len(peers))


def remote(src, dst, send, recv, device):
    copy = pltpu.make_async_remote_copy(
        src_ref=src, dst_ref=dst, send_sem=send, recv_sem=recv, device_id=device, device_id_type=MESH
    )
    copy.start()
    return copy


def around(axis):
    count = {"line": NLINE, "cross": NCROSS}[axis]
    me = lax.axis_index(axis)
    return me, [lax.rem(me + d, count) for d in range(1, count)]


def elimination(axial, sound, lead, tail, first, second, inverse, corners, half):
    lanes = pl.ds(half * 128, 128)
    zero = sound[0, :, lanes] * 0.0

    def body(i, carried):
        speed, wave = axial[i, :, lanes], sound[i, :, lanes]
        rho = jnp.abs(speed) + wave
        after = []
        for s in range(3):
            e1, p1, q1, q2, a1, a2, b1, b2, aa, ab, bb = carried[s]
            r = 1.0 / (rho + 0.5 * jnp.abs(speed + SIGMA[s] * wave))
            inv = 1.0 / ((MID + r) - TWO * q2 - e1 * p1)
            e = ONE - TWO * p1
            p = e * inv
            q = TWO * inv
            a = jnp.where(i == 0, 1.0, 0.0) - p1 * a1 - q2 * a2
            b = jnp.where(i == 1, 1.0, 0.0) - p1 * b1 - q2 * b2
            ai, bi = a * inv, b * inv
            lead[s, i, :, lanes], tail[s, i, :, lanes] = p, q
            first[s, i, :, lanes], second[s, i, :, lanes], inverse[s, i, :, lanes] = a, b, r
            after.append((e, p, q, q1, a, a1, b, b1, aa + ai * a, ab + ai * b, bb + bi * b))
        return tuple(after)

    done = lax.fori_loop(0, CL, body, (((zero,) * 11),) * 3, unroll=4)
    for s in range(3):
        _, _, q1, q2, a1, a2, b1, b2, aa, ab, bb = done[s]
        inv1, inv2, p2 = 0.5 * q1, 0.5 * q2, lead[s, CL - 2, :, lanes]
        entries = (
            aa,
            ab,
            bb,
            a2 * inv2 - a1 * p2 * inv1,
            a1 * inv1,
            b2 * inv2 - b1 * p2 * inv1,
            b1 * inv1,
            inv2 + p2 * p2 * inv1,
            -p2 * inv1,
            inv1,
        )
        for m, entry in enumerate(entries):
            corners[:, 3 * m + s, lanes] = entry


def front_kernel(
    base, frac, cell, live, axial, sound, crossing, state,
    lists, cells, above, below, before, after, line_in, cross_in, lead_out, tail_out, first_out, second_out,
    inverse_out, corners_in,
    packed, inbox, line_out, cross_out, edges, values, left, right, lead, tail, first, second, inverse, corners,
    ask_send, ask_recv, fixed_send, fixed_recv, corner_send, corner_recv, value_send, own_recv, side_recv,
    relay_send, relay_recv, kept,
):
    me, peers = around("cross")
    row, others = around("line")
    down, up = others[0], others[-1]
    rightward, leftward = peers[0], peers[-1]

    for half in range(2):
        lanes = pl.ds(half * 128, 128)
        packed[:, half, :] = base[:, lanes].astype(F32)
        for q in range(3):
            packed[:, 2 * q + 2 + half, :] = frac[q, :, lanes]
    inbox[me] = packed[me]
    slot = lax.broadcasted_iota(jnp.int32, (1, CAP), 1)
    for p in range(NCROSS):
        cells[0, p : p + 1, :] = jnp.where(slot < live[p], cell[p : p + 1, :], -1)
    line_out[0] = axial[0]
    line_out[1] = sound[0]
    line_out[2] = axial[CL - 1]
    line_out[3] = sound[CL - 1]
    cross_out[0] = crossing[:, 0, :]
    cross_out[1] = crossing[:, CJ - 1, :]

    greet([(row, p) for p in peers] + [(r, me) for r in others])
    asks = [
        remote(packed.at[p], inbox.at[me], ask_send, ask_recv.at[d], (row, p)) for d, p in enumerate(peers)
    ]
    fixed = []

    def fix(source, target, device):
        m = len(fixed)
        fixed.append(remote(source, target, fixed_send.at[m], fixed_recv.at[m], device))

    fix(cells.at[0], cells.at[2], (row, leftward))
    fix(cells.at[0], cells.at[1], (row, rightward))
    fix(cells.at[0], cells.at[4], (up, me))
    fix(cells.at[0], cells.at[3], (down, me))
    fix(line_out.at[pl.ds(0, 2)], line_in.at[pl.ds(2, 2)], (up, me))
    fix(line_out.at[pl.ds(2, 2)], line_in.at[pl.ds(0, 2)], (down, me))
    fix(cross_out.at[0], cross_in.at[1], (row, leftward))
    fix(cross_out.at[1], cross_in.at[0], (row, rightward))
    fix(state.at[:, pl.ds(0, 2)], below, (up, me))
    fix(state.at[:, pl.ds(CL - 2, 2)], above, (down, me))

    @pl.loop(0, NV)
    def _(v):
        for j in range(2):
            edges[0, v, j] = state[v, :, j, :]
            edges[1, v, j] = state[v, :, CJ - 2 + j, :]

    fix(edges.at[0], after, (row, leftward))
    fix(edges.at[1], before, (row, rightward))

    @pl.loop(0, NV)
    def _(v):
        flipped = state[v].reshape(CL * CJ, NK).T
        high = flipped.astype(BF16)
        low = (flipped - high.astype(F32)).astype(BF16)
        left[v, :, 0:512] = high
        left[v, :, 512:1024] = low
        left[v, :, 1024:1536] = high

    corners[...] = jnp.zeros(corners.shape, F32)
    for half in range(2):
        elimination(axial, sound, lead, tail, first, second, inverse, corners, half)
    shared = [
        remote(corners.at[r], corners_in.at[row], corner_send.at[d], corner_recv.at[d], (r, me))
        for d, r in enumerate(others)
    ]
    stores = [pltpu.make_async_copy(corners.at[row], corners_in.at[row], kept.at[5])]
    for m, (here, there) in enumerate(
        ((lead, lead_out), (tail, tail_out), (first, first_out), (second, second_out), (inverse, inverse_out))
    ):
        stores.append(pltpu.make_async_copy(here, there, kept.at[m]))
    for store in stores:
        store.start()

    def relay(d):
        donor = lax.rem(me + NCROSS - d, NCROSS)
        for m, device in enumerate(((down, me), (up, me))):
            remote(lists.at[0, donor], lists.at[3 + m, donor], relay_send.at[m], relay_recv.at[m], device)

    def own_arrival(d):
        donor = lax.rem(me + NCROSS - d, NCROSS)
        pltpu.make_async_remote_copy(
            src_ref=values.at[donor], dst_ref=lists.at[0, donor], send_sem=value_send.at[0],
            recv_sem=own_recv.at[d - 1], device_id=(row, donor), device_id_type=MESH,
        ).wait_recv()

    lag = 3

    @pl.loop(0, NCROSS)
    def _(d):
        p = lax.rem(me + d, NCROSS)

        @pl.when(d > 0)
        def _():
            pltpu.make_async_remote_copy(
                src_ref=packed.at[p], dst_ref=inbox.at[p], send_sem=ask_send, recv_sem=ask_recv.at[15 - d],
                device_id=(row, p), device_id_type=MESH,
            ).wait_recv()

        asked = inbox[p]

        def field(q):
            return jnp.concatenate([asked[2 * q : 2 * q + 1, :], asked[2 * q + 1 : 2 * q + 2, :]], 1)

        origin = field(0).astype(jnp.int32)
        fx, fy, fz = field(1), field(2), field(3)
        gx, gy, gz = 1.0 - fx, 1.0 - fy, 1.0 - fz
        lowest = lax.shift_right_logical(origin, 8)
        depth = lax.bitwise_and(origin, 255)
        away = lax.broadcasted_iota(jnp.int32, (512, CAP), 0) - lowest
        weight = jnp.where(
            away == 0,
            gx * gy,
            jnp.where(away == 1, gx * fy, jnp.where(away == 8, fx * gy, jnp.where(away == 9, fx * fy, 0.0))),
        )
        high = weight.astype(BF16)
        low = (weight - high.astype(F32)).astype(BF16)
        right[0:512] = high
        right[512:1024] = high
        right[1024:1536] = low
        past = lax.broadcasted_iota(jnp.int32, (NK, CAP), 0) - depth
        along = jnp.where(past == 0, gz, jnp.where(past == 1, fz, 0.0))
        rows = []
        for v in range(NV):
            mixed = jnp.dot(left[v], right[...], preferred_element_type=F32)
            rows.append(jnp.sum(mixed * along, axis=0, keepdims=True))
        result = jnp.concatenate(rows + [jnp.zeros((3, CAP), F32)], 0)
        values[p] = result

        @pl.when(d == 0)
        def _():
            lists[0, me] = result

        @pl.when(d > 0)
        def _():
            remote(values.at[p], lists.at[0, me], value_send.at[0], own_recv.at[d - 1], (row, p))

        @pl.when(d == 15)
        def _():
            lists[1, me] = result

        @pl.when(d != 15)
        def _():
            q = lax.rem(p + 1, NCROSS)
            remote(values.at[p], lists.at[1, me], value_send.at[1], side_recv.at[0], (row, q))

        @pl.when(d == 1)
        def _():
            lists[2, me] = result

        @pl.when(d != 1)
        def _():
            q = lax.rem(p + NCROSS - 1, NCROSS)
            remote(values.at[p], lists.at[2, me], value_send.at[2], side_recv.at[1], (row, q))

        @pl.when(d == lag)
        def _():
            relay(0)

        @pl.when(d > lag)
        def _():
            own_arrival(d - lag)
            relay(d - lag)

    for d in range(NCROSS - lag, NCROSS):
        own_arrival(d)
        relay(d)

    def settle(source, target, send, recv, device):
        return pltpu.make_async_remote_copy(
            src_ref=source, dst_ref=target, send_sem=send, recv_sem=recv, device_id=device, device_id_type=MESH
        )

    most = pl.ds(0, 15)
    settle(packed.at[most], inbox.at[most], ask_send, ask_recv.at[0], (row, rightward)).wait_send()
    for m in range(3):
        wait = settle(
            values.at[most], lists.at[m, most], value_send.at[m], side_recv.at[max(m - 1, 0)], (row, rightward)
        )
        wait.wait_send()
        if m:
            wait.wait_recv()
    for m in range(2):
        settle(lists.at[0], lists.at[3 + m], relay_send.at[m], relay_recv.at[m], (down, me)).wait()
    for copy in fixed + shared + stores:
        copy.wait()


def front(base, frac, cell, live, axial, sound, crossing, state):
    sems = pltpu.SemaphoreType.DMA
    full = jax.ShapeDtypeStruct((3, CL, CJ, NK), F32)
    ends = jax.ShapeDtypeStruct((NV, 2, CJ, NK), F32)
    edge = jax.ShapeDtypeStruct((NV, 2, CL, NK), F32)
    part = pltpu.VMEM((3, CL, CJ, NK), F32)
    return pl.pallas_call(
        front_kernel,
        out_shape=(
            jax.ShapeDtypeStruct((5, NCROSS, 8, CAP), F32),
            jax.ShapeDtypeStruct((5, NCROSS, CAP), jnp.int32),
            ends,
            ends,
            edge,
            edge,
            jax.ShapeDtypeStruct((4, CJ, NK), F32),
            jax.ShapeDtypeStruct((2, CL, NK), F32),
            full,
            full,
            full,
            full,
            full,
            jax.ShapeDtypeStruct((NLINE, 32, NK), F32),
        ),
        in_specs=[VMEM_SPEC] * 3 + [SMEM_SPEC] + [VMEM_SPEC] * 4,
        out_specs=(VMEM_SPEC,) * 2 + (ANY_SPEC,) * 12,
        scratch_shapes=[
            pltpu.VMEM((NCROSS, 8, 128), F32),
            pltpu.VMEM((NCROSS, 8, 128), F32),
            pltpu.VMEM((4, CJ, NK), F32),
            pltpu.VMEM((2, CL, NK), F32),
            pltpu.VMEM((2, NV, 2, CL, NK), F32),
            pltpu.VMEM((NCROSS, 8, CAP), F32),
            pltpu.VMEM((NV, NK, 1536), BF16),
            pltpu.VMEM((1536, CAP), BF16),
            part,
            part,
            part,
            part,
            part,
            pltpu.VMEM((CJ, 32, NK), F32),
            sems,
            sems((15,)),
            sems((12,)),
            sems((12,)),
            sems((7,)),
            sems((7,)),
            sems((3,)),
            sems((15,)),
            sems((2,)),
            sems((2,)),
            sems((2,)),
            sems((6,)),
        ],
        compiler_params=pltpu.CompilerParams(collective_id=0, has_side_effects=True, vmem_limit_bytes=FRONT),
        name="front",
    )(base, frac, cell, live, axial, sound, crossing, state)


def place_values(values, cells, m, rows, spread, along):
    count = rows.shape[0]
    for p in range(NCROSS):
        lanes = slice(p * CAP, (p + 1) * CAP)
        hit = rows == lax.shift_right_arithmetic(cells[m, p : p + 1, :], 8)
        picked = jnp.where(hit, 1.0, 0.0).astype(BF16)
        for v in range(NV):
            here = values[m, p, v : v + 1, :]
            high = here.astype(BF16)
            low = (here - high.astype(F32)).astype(BF16)
            spread[v * count : (v + 1) * count, lanes] = picked * high
            spread[(NV + v) * count : (NV + v + 1) * count, lanes] = picked * low
        spread[2 * NV * count : (2 * NV + 1) * count, lanes] = picked
    placed = lax.dot_general(
        spread[0 : 11 * count, :], along[...], (((1,), (1,)), ((), ())), preferred_element_type=F32
    )
    taken = placed[2 * NV * count :] > 0.5
    fresh = [
        placed[v * count : (v + 1) * count] + placed[(NV + v) * count : (NV + v + 1) * count] for v in range(NV)
    ]
    return taken, fresh


def depths(cells, m, along):
    for p in range(NCROSS):
        depth = lax.bitwise_and(cells[m, p : p + 1, :], 255)
        hit = lax.broadcasted_iota(jnp.int32, (NK, CAP), 0) == depth
        along[:, p * CAP : (p + 1) * CAP] = jnp.where(hit, 1.0, 0.0).astype(BF16)


def middle_kernel(
    where, values, cells, state, above, below, before_in, after_in, axial, sound, crossing, line_halo, cross_halo,
    lead_in, tail_in, first_in, second_in, inverse_in,
    out, fringe, ends,
    full, before, after, crosses_by, speeds, waves, spread, along, lead, tail, first, second, inverse, loads,
):
    line, cross = where[0], where[1]
    copies = []
    for m, (there, here) in enumerate(
        ((lead_in, lead), (tail_in, tail), (first_in, first), (second_in, second), (inverse_in, inverse))
    ):
        copies.append(pltpu.make_async_copy(there, here, loads.at[m]))
        copies[-1].start()

    def inside(flag, value):
        return jnp.where(flag, value, 0.0)

    depths(cells, 0, along)

    @pl.loop(0, 8)
    def _(t):
        rows = lax.broadcasted_iota(jnp.int32, (64, CAP), 0) + t * 64
        taken, fresh = place_values(values, cells, 0, rows, spread, along)
        for v in range(NV):
            old = state[v, pl.ds(t * 8, 8)].reshape(64, NK)
            now = jnp.where(taken, fresh[v], old).reshape(8, CJ, NK)
            full[v, pl.ds(2 + t * 8, 8)] = now
            fringe[v, pl.ds(t * 8, 8)] = now

    for m, column, source, target, flag in (
        (1, CJ - 2, before_in, before, cross > 0),
        (2, 0, after_in, after, cross < NCROSS - 1),
    ):
        depths(cells, m, along)

        @pl.loop(0, 2)
        def _(j):
            rows = lax.broadcasted_iota(jnp.int32, (CL, CAP), 0) * CJ + column + j
            taken, fresh = place_values(values, cells, m, rows, spread, along)
            for v in range(NV):
                now = inside(flag, jnp.where(taken, fresh[v], source[v, j]))
                target[0, v, j] = now[:, 0:128]
                target[1, v, j] = now[:, 128:256]

    for m, first_row, source, start, flag in (
        (3, CL - 2, above, 0, line > 0),
        (4, 0, below, CL + 2, line < NLINE - 1),
    ):
        depths(cells, m, along)
        rows = lax.broadcasted_iota(jnp.int32, (16, CAP), 0) + first_row * CJ
        taken, fresh = place_values(values, cells, m, rows, spread, along)
        for v in range(NV):
            now = jnp.where(taken, fresh[v], source[v].reshape(16, NK))
            full[v, pl.ds(start, 2)] = inside(flag, now).reshape(2, CJ, NK)

    for half in range(2):
        crosses_by[half] = cross_halo[:, :, pl.ds(half * 128, 128)]
    speeds[pl.ds(1, CL)] = axial[...]
    waves[pl.ds(1, CL)] = sound[...]
    speeds[0], waves[0] = line_halo[0], line_halo[1]
    speeds[CL + 1], waves[CL + 1] = line_halo[2], line_halo[3]
    for copy in copies:
        copy.wait()

    ends[...] = jnp.zeros(ends.shape, F32)
    column = lax.broadcasted_iota(jnp.int32, (CJ, 128), 0)
    for half in range(2):
        lanes = pl.ds(half * 128, 128)
        zero = sound[0, :, lanes] * 0.0

        def body(i, carried):
            speed, wave, crosses = axial[i, :, lanes], sound[i, :, lanes], crossing[i, :, lanes]
            rho = jnp.abs(speed) + wave
            speed_up, wave_up = speeds[i, :, lanes], waves[i, :, lanes]
            speed_down, wave_down = speeds[i + 2, :, lanes], waves[i + 2, :, lanes]
            row = pl.ds(i, 1)
            cross_left = jnp.where(column == 0, crosses_by[half, 0, row, :], pltpu.roll(crosses, 1, 0))
            cross_right = jnp.where(column == CJ - 1, crosses_by[half, 1, row, :], pltpu.roll(crosses, CJ - 1, 0))
            following = []
            for v in range(NV):
                s = SETS[v]
                y1, y2, low, high = carried[v]
                q = full[v, i + 2, :, lanes]
                up, down = full[v, i + 1, :, lanes], full[v, i + 3, :, lanes]
                fourth = full[v, i, :, lanes] + full[v, i + 4, :, lanes] - 4.0 * (up + down) + 6.0 * q
                l2, l1 = before[half, v, 0, row, :], before[half, v, 1, row, :]
                r1, r2 = after[half, v, 0, row, :], after[half, v, 1, row, :]
                left1 = jnp.where(column == 0, l1, pltpu.roll(q, 1, 0))
                left2 = jnp.where(column == 0, l2, jnp.where(column == 1, l1, pltpu.roll(q, 2, 0)))
                right1 = jnp.where(column == CJ - 1, r1, pltpu.roll(q, CJ - 1, 0))
                right2 = jnp.where(column == CJ - 1, r2, jnp.where(column == CJ - 2, r1, pltpu.roll(q, CJ - 2, 0)))
                fourth_cross = left2 + right2 - 4.0 * (left1 + right1) + 6.0 * q
                lam_up = speed_up + SIGMA[s] * wave_up
                lam_down = speed_down + SIGMA[s] * wave_down
                source = (
                    -4.0 * (lam_down * down - lam_up * up)
                    - 4.0 * (cross_right * right1 - cross_left * left1)
                    - 8.0 * rho * (fourth + 0.03125 * fourth_cross)
                )
                p1 = lead[s, jnp.maximum(i - 1, 0), :, lanes]
                q2 = tail[s, jnp.maximum(i - 2, 0), :, lanes]
                y = source * inverse[s, i, :, lanes] - p1 * y1 - q2 * y2
                out[v, i, :, lanes] = y
                t = y * (0.5 * tail[s, i, :, lanes])
                following.append((y, y1, low + first[s, i, :, lanes] * t, high + second[s, i, :, lanes] * t))
            return tuple(following)

        done = lax.fori_loop(0, CL, body, (((zero,) * 4),) * NV, unroll=2)
        for v in range(NV):
            s = SETS[v]
            y1, y2, low, high = done[v]
            last = 0.5 * tail[s, CL - 1, :, lanes] * y1
            ends[:, v, lanes] = low
            ends[:, 8 + v, lanes] = high
            ends[:, 16 + v, lanes] = 0.5 * tail[s, CL - 2, :, lanes] * y2 - lead[s, CL - 2, :, lanes] * last
            ends[:, 24 + v, lanes] = last


def middle(place, values, cells, state, halos, axial, sound, crossing, line_halo, cross_halo, factors):
    block = jax.ShapeDtypeStruct((NV, CL, CJ, NK), F32)
    part = pltpu.VMEM((3, CL, CJ, NK), F32)
    return pl.pallas_call(
        middle_kernel,
        out_shape=(block, block, jax.ShapeDtypeStruct((CJ, 32, NK), F32)),
        in_specs=[SMEM_SPEC] + [VMEM_SPEC] * 12 + [ANY_SPEC] * 5,
        out_specs=(VMEM_SPEC,) * 3,
        scratch_shapes=[
            pltpu.VMEM((NV, CL + 4, CJ, NK), F32),
            pltpu.VMEM((2, NV, 2, CL, 128), F32),
            pltpu.VMEM((2, NV, 2, CL, 128), F32),
            pltpu.VMEM((2, 2, CL, 128), F32),
            pltpu.VMEM((CL + 2, CJ, NK), F32),
            pltpu.VMEM((CL + 2, CJ, NK), F32),
            pltpu.VMEM((11 * 64, NCROSS * CAP), BF16),
            pltpu.VMEM((NK, NCROSS * CAP), BF16),
            part,
            part,
            part,
            part,
            part,
            pltpu.SemaphoreType.DMA((5,)),
        ],
        compiler_params=pltpu.CompilerParams(vmem_limit_bytes=MIDDLE),
        name="middle",
    )(place, values, cells, state, *halos, axial, sound, crossing, line_halo, cross_halo, *factors)


def times(m, n):
    a, b, c, d = m
    e, f, g, h = n
    return (a * e + b * g, a * f + b * h, c * e + d * g, c * f + d * h)


def apply(m, x):
    return (m[0] * x[0] + m[1] * x[1], m[2] * x[0] + m[3] * x[1])


def right_upper(m):
    return (TWO * m[0], ONE * m[0] + TWO * m[1], TWO * m[2], ONE * m[2] + TWO * m[3])


def right_lower(m):
    return (TWO * m[0] + ONE * m[1], TWO * m[1], TWO * m[2] + ONE * m[3], TWO * m[3])


def plus(m, n):
    return tuple(a + b for a, b in zip(m, n))


def minus(m, n):
    return tuple(a - b for a, b in zip(m, n))


def interface_kernel(mine, corners, out, ends, forces, send, recv, own):
    column = lax.axis_index("cross")
    me, peers = around("line")
    greet([(p, column) for p in peers])

    def trade(source, target, m):
        copies = [
            remote(source.at[p], target.at[me], send.at[m, d], recv.at[m, d], (p, column)) for d, p in enumerate(peers)
        ]
        copies.append(pltpu.make_async_copy(source.at[me], target.at[me], own.at[m]))
        copies[-1].start()
        for copy in copies:
            copy.wait()

    trade(mine, ends, 0)
    variable = lax.broadcasted_iota(jnp.int32, (8, NK), 0)

    def corner(l, m):
        rows = [corners[l, 3 * m + s : 3 * m + s + 1, :] for s in range(3)]
        return jnp.where(variable == 0, rows[0], jnp.where(variable == 4, rows[2], rows[1]))

    steps = []
    p = m = None
    for l in range(NLINE):
        c = [corner(l, k) for k in range(10)]
        heads = (c[0], c[1], c[1], c[2])
        cross = (c[3], c[4], c[5], c[6])
        back = (c[3], c[5], c[4], c[6])
        tails = (c[7], c[8], c[8], c[9])
        ya = (ends[l, 0:8, :], ends[l, 8:16, :])
        yb = (ends[l, 16:24, :], ends[l, 24:32, :])
        if l == 0:
            inner, reach = ya, right_lower(cross)
            p, m = yb, right_lower(tails)
        else:
            heads_u, back_u = right_upper(heads), right_upper(back)
            t = times(heads_u, m)
            g = (1.0 - t[0], -t[1], -t[2], 1.0 - t[3])
            scale = 1.0 / (g[0] * g[3] - g[1] * g[2])
            g = (g[3] * scale, -g[1] * scale, -g[2] * scale, g[0] * scale)
            inner = apply(g, minus(ya, apply(heads_u, p)))
            reach = right_lower(times(g, cross))
            back_um = times(back_u, m)
            p = plus(minus(yb, apply(back_u, p)), apply(back_um, inner))
            m = plus(right_lower(tails), times(back_um, reach))
        steps.append((inner, reach, p, m))
    a = None
    for l in reversed(range(NLINE)):
        inner, reach, _, _ = steps[l]
        zero = ends[0, 0:8, :] * 0.0
        if l == NLINE - 1:
            beta = (zero, zero)
            a = inner
        else:
            beta = (TWO * a[0], ONE * a[0] + TWO * a[1])
            a = minus(inner, apply(reach, a))
        if l == 0:
            alpha = (zero, zero)
        else:
            _, _, p, m = steps[l - 1]
            b = minus(p, apply(m, a))
            alpha = (TWO * b[0] + ONE * b[1], TWO * b[1])
        forces[l, 0:8, :] = alpha[0]
        forces[l, 8:16, :] = alpha[1]
        forces[l, 16:24, :] = beta[0]
        forces[l, 24:32, :] = beta[1]
    trade(forces, out, 1)


def interface(ends, corners):
    return pl.pallas_call(
        interface_kernel,
        out_shape=jax.ShapeDtypeStruct((CJ, 32, NK), F32),
        in_specs=[VMEM_SPEC] * 2,
        out_specs=VMEM_SPEC,
        scratch_shapes=[
            pltpu.VMEM((NLINE, 32, NK), F32),
            pltpu.VMEM((NLINE, 32, NK), F32),
            pltpu.SemaphoreType.DMA((2, 7)),
            pltpu.SemaphoreType.DMA((2, 7)),
            pltpu.SemaphoreType.DMA((2,)),
        ],
        compiler_params=pltpu.CompilerParams(collective_id=1, has_side_effects=True),
        name="interface",
    )(ends, corners)


def backward_kernel(forces, eliminated, state, lead, tail, first, second, out):
    def forced(v, i):
        s = SETS[v]
        alpha0, alpha1 = forces[:, v, :], forces[:, 8 + v, :]
        return eliminated[v, i] - first[s, i] * alpha0 - second[s, i] * alpha1

    start = []
    for v in range(NV):
        s = SETS[v]
        beta0, beta1 = forces[:, 16 + v, :], forces[:, 24 + v, :]
        p2 = lead[s, CL - 2]
        last = (forced(v, CL - 1) - beta1 + p2 * beta0) * (0.5 * tail[s, CL - 1])
        prior = (forced(v, CL - 2) - beta0) * (0.5 * tail[s, CL - 2]) - p2 * last
        out[v, CL - 1] = state[v, CL - 1] + last
        out[v, CL - 2] = state[v, CL - 2] + prior
        start.append((prior, last))

    def body(t, carried):
        i = CL - 3 - t
        following = []
        for v in range(NV):
            s = SETS[v]
            x1, x2 = carried[v]
            q = tail[s, i]
            x = (0.5 * forced(v, i) - x2) * q - lead[s, i] * x1
            out[v, i] = state[v, i] + x
            following.append((x, x1))
        return tuple(following)

    lax.fori_loop(0, CL - 2, body, tuple(start), unroll=2)


def backward(forces, eliminated, state, lead, tail, first, second):
    def lanes(*sizes):
        zeros = (0,) * len(sizes)
        return pl.BlockSpec(sizes + (128,), lambda h: zeros + (h,))

    return pl.pallas_call(
        backward_kernel,
        grid=(2,),
        out_shape=jax.ShapeDtypeStruct((NV, CL, CJ, NK), F32),
        in_specs=[lanes(CJ, 32), lanes(NV, CL, CJ), lanes(NV, CL, CJ)] + [lanes(3, CL, CJ)] * 4,
        out_specs=lanes(NV, CL, CJ),
        compiler_params=pltpu.CompilerParams(vmem_limit_bytes=BIG),
        name="backward",
    )(forces, eliminated, state, lead, tail, first, second)


def on_device(
    state, axial_speed, sound_speed, cross_speed, donor_base, donor_frac, fringe_cell, live_count
):
    place = jnp.stack([lax.axis_index("line"), lax.axis_index("cross")]).astype(jnp.int32)
    lists, cells, above, below, before, after, line_halo, cross_halo, *factors, corners = front(
        donor_base.reshape(NCROSS, CAP),
        donor_frac.reshape(3, NCROSS, CAP),
        fringe_cell.reshape(NCROSS, CAP),
        live_count.reshape(NCROSS),
        axial_speed,
        sound_speed,
        cross_speed,
        state,
    )
    eliminated, fringe, ends = middle(
        place,
        lists,
        cells,
        state,
        (above, below, before, after),
        axial_speed,
        sound_speed,
        cross_speed,
        line_halo,
        cross_halo,
        factors,
    )
    return backward(interface(ends, corners), eliminated, fringe, *factors[:4])


def solution(mesh):
    in_specs = (
        P(None, "line", "cross", None),
        P("line", "cross", None),
        P("line", "cross", None),
        P("line", "cross", None),
        P("line", "cross", None, None),
        P("line", "cross", None, None, None),
        P("line", "cross", None, None),
        P("line", "cross", None),
    )
    out_specs = P(None, "line", "cross", None)
    return jax.shard_map(
        on_device, mesh=mesh, in_specs=in_specs, out_specs=out_specs, check_vma=False
    )
```

```python
import jax
import jax.numpy as jnp
from jax import lax
from jax.experimental import pallas as pl
from jax.experimental.pallas import tpu as pltpu
from jax.sharding import PartitionSpec as P

MESH = pl.DeviceIdType.MESH
F32 = jnp.float32
BF16 = jnp.bfloat16
NV, CL, CJ, NK, CAP = 5, 64, 8, 256, 256
NLINE, NCROSS = 8, 16
SETS = (0, 1, 1, 1, 2)
SIGMA = (-1.0, 0.0, 1.0)
ONE, TWO, MID = -264.0, 2.0, 524.0
F8 = jnp.float8_e4m3fn
LIMIT = 62 * 1024 * 1024
TRANSPOSED = (((1,), (1,)), ((), ()))

SMEM_SPEC = pl.BlockSpec(memory_space=pltpu.SMEM)
HBM_SPEC = pl.BlockSpec(memory_space=pltpu.HBM)


def remote(src, dst, send, recv, device):
    copy = pltpu.make_async_remote_copy(
        src_ref=src, dst_ref=dst, send_sem=send, recv_sem=recv, device_id=device, device_id_type=MESH
    )
    copy.start()
    return copy


def around(axis):
    count = {"line": NLINE, "cross": NCROSS}[axis]
    me = lax.axis_index(axis)
    return me, [lax.rem(me + d, count) for d in range(1, count)]


def build_tables(full, tables):
    odd = lax.bitwise_and(lax.broadcasted_iota(jnp.int32, (CL // 2, CJ, NK), 1), 1) == 1

    @pl.loop(0, NV)
    def _(v):
        pairs = full[v, pl.ds(2, CL)].reshape(CL // 2, 2, CJ, NK)
        for a in range(2):
            high = pairs[:, a].astype(BF16).astype(F32)
            low = pairs[:, a] - high
            for b in range(2):
                if b == 0:
                    mixed = jnp.where(odd, pltpu.roll(low, 1, 1), high)
                else:
                    mixed = jnp.where(odd, high, pltpu.roll(low, CJ - 1, 1))
                tables[2 * a + b, v] = mixed.reshape(256, NK).T.astype(BF16)


def read_request(asked):
    def field(q):
        return jnp.concatenate([asked[2 * q : 2 * q + 1, :], asked[2 * q + 1 : 2 * q + 2, :]], 1)

    origin = field(0).astype(jnp.int32)
    row = lax.shift_right_logical(origin, 11)
    column = lax.bitwise_and(lax.shift_right_logical(origin, 8), 7)
    return row, column, lax.bitwise_and(origin, 255), field(1), field(2), field(3)


def build_hots(asked, hots, slot):
    row, column, _, _, _, _ = read_request(asked)
    place = lax.shift_right_logical(lax.broadcasted_iota(jnp.int32, (256, CAP), 0), 1)
    for a in range(2):
        for b in range(2):
            corner = lax.shift_right_logical(row + 1 - a, 1) * 4 + lax.shift_right_logical(column + 1 - b, 1)
            hots[slot, 2 * a + b] = jnp.where(place == corner, 1.0, 0.0).astype(BF16)


def donor_products(asked, tables, hots, slot):
    row, column, depth, fx, fy, fz = read_request(asked)
    even_row = lax.bitwise_and(row, 1) == 0
    even_column = lax.bitwise_and(column, 1) == 0
    gx, gy, gz = 1.0 - fx, 1.0 - fy, 1.0 - fz
    along_x = (jnp.where(even_row, gx, fx), jnp.where(even_row, fx, gx))
    along_y = (jnp.where(even_column, gy, fy), jnp.where(even_column, fy, gy))
    past = lax.broadcasted_iota(jnp.int32, (NK, CAP), 0) - depth
    along_z = jnp.where(past == 0, gz, jnp.where(past == 1, fz, 0.0))
    sums = [0.0] * NV
    for a in range(2):
        for b in range(2):
            weight = along_x[a] * along_y[b]
            rows = tables[2 * a + b].reshape(NV * NK, 256)
            mixed = jnp.dot(rows, hots[slot, 2 * a + b], preferred_element_type=F32)
            for v in range(NV):
                sums[v] += weight * jnp.sum(mixed[v * NK : (v + 1) * NK] * along_z, axis=0, keepdims=True)
    return jnp.concatenate(sums + [jnp.zeros((3, CAP), F32)], 0)


def build_depths(cells, m, wide, narrow):
    for p in range(NCROSS):
        depth = lax.bitwise_and(cells[m, p : p + 1, :], 255)
        hit = jnp.where(lax.broadcasted_iota(jnp.int32, (NK, CAP), 0) == depth, 1.0, 0.0)
        wide[:, p * CAP : (p + 1) * CAP] = hit.astype(BF16)
        narrow[:, p * CAP : (p + 1) * CAP] = hit.astype(F8)


def place_values(values, cells, m, rows, wide, narrow, high_part, low_part):
    count = rows.shape[0]
    peak = jnp.maximum(jnp.max(jnp.abs(values[m]), axis=(0, 1, 2), keepdims=True)[0], 1e-30)
    scale = 65536.0 / peak
    for p in range(NCROSS):
        lanes = slice(p * CAP, (p + 1) * CAP)
        hit = rows == lax.shift_right_arithmetic(cells[m, p : p + 1, :], 8)
        picked = jnp.where(hit, 1.0, 0.0).astype(BF16)
        for v in range(NV):
            here = values[m, p, v : v + 1, :]
            high = here.astype(BF16)
            low = ((here - high.astype(F32)) * scale).astype(BF16)
            high_part[v * count : (v + 1) * count, lanes] = picked * high
            low_part[v * count : (v + 1) * count, lanes] = (picked * low).astype(F8)
        low_part[NV * count : (NV + 1) * count, lanes] = picked.astype(F8)
    high = lax.dot_general(high_part[...], wide[...], TRANSPOSED, preferred_element_type=F32)
    low = lax.dot_general(low_part[...], narrow[...], TRANSPOSED, preferred_element_type=F32)
    unscale = peak * (1.0 / 65536.0)
    fresh = [
        high[v * count : (v + 1) * count] + low[v * count : (v + 1) * count] * unscale for v in range(NV)
    ]
    return low[NV * count :] > 0.5, fresh


def elimination(axial, sound, lead, tail, first, second, inverse, corners, half):
    lanes = pl.ds(half * 128, 128)
    zero = sound[0, :, lanes] * 0.0

    def body(i, carried):
        speed, wave = axial[i + 1, :, lanes], sound[i + 1, :, lanes]
        rho = jnp.abs(speed) + wave
        after = []
        for s in range(3):
            e1, p1, q1, q2, a1, a2, b1, b2, aa, ab, bb = carried[s]
            r = 1.0 / (rho + 0.5 * jnp.abs(speed + SIGMA[s] * wave))
            inv = 1.0 / ((MID + r) - TWO * q2 - e1 * p1)
            e = ONE - TWO * p1
            p = e * inv
            q = TWO * inv
            a = jnp.where(i == 0, 1.0, 0.0) - p1 * a1 - q2 * a2
            b = jnp.where(i == 1, 1.0, 0.0) - p1 * b1 - q2 * b2
            ai, bi = a * inv, b * inv
            lead[s, i, :, lanes], tail[s, i, :, lanes] = p, q
            first[s, i, :, lanes], second[s, i, :, lanes], inverse[s, i, :, lanes] = a, b, r
            after.append((e, p, q, q1, a, a1, b, b1, aa + ai * a, ab + ai * b, bb + bi * b))
        return tuple(after)

    done = lax.fori_loop(0, CL, body, (((zero,) * 11),) * 3, unroll=4)
    for s in range(3):
        _, _, q1, q2, a1, a2, b1, b2, aa, ab, bb = done[s]
        inv1, inv2, p2 = 0.5 * q1, 0.5 * q2, lead[s, CL - 2, :, lanes]
        entries = (
            aa,
            ab,
            bb,
            a2 * inv2 - a1 * p2 * inv1,
            a1 * inv1,
            b2 * inv2 - b1 * p2 * inv1,
            b1 * inv1,
            inv2 + p2 * p2 * inv1,
            -p2 * inv1,
            inv1,
        )
        for m, entry in enumerate(entries):
            corners[:, 3 * m + s, lanes] = entry


def times(m, n):
    a, b, c, d = m
    e, f, g, h = n
    return (a * e + b * g, a * f + b * h, c * e + d * g, c * f + d * h)


def apply(m, x):
    return (m[0] * x[0] + m[1] * x[1], m[2] * x[0] + m[3] * x[1])


def right_upper(m):
    return (TWO * m[0], ONE * m[0] + TWO * m[1], TWO * m[2], ONE * m[2] + TWO * m[3])


def right_lower(m):
    return (TWO * m[0] + ONE * m[1], TWO * m[1], TWO * m[2] + ONE * m[3], TWO * m[3])


def plus(m, n):
    return tuple(a + b for a, b in zip(m, n))


def minus(m, n):
    return tuple(a - b for a, b in zip(m, n))


def solve_interface(ends, corners, forces):
    variable = lax.broadcasted_iota(jnp.int32, (NV, NK), 0)

    def corner(l, m):
        rows = [corners[l, 3 * m + s : 3 * m + s + 1, :] for s in range(3)]
        return jnp.where(variable == 0, rows[0], jnp.where(variable == 4, rows[2], rows[1]))

    steps = []
    p = m = None
    for l in range(NLINE):
        c = [corner(l, k) for k in range(10)]
        heads = (c[0], c[1], c[1], c[2])
        cross = (c[3], c[4], c[5], c[6])
        back = (c[3], c[5], c[4], c[6])
        tails = (c[7], c[8], c[8], c[9])
        ya = (ends[l, 0:5, :], ends[l, 5:10, :])
        yb = (ends[l, 10:15, :], ends[l, 15:20, :])
        if l == 0:
            inner, reach = ya, right_lower(cross)
            p, m = yb, right_lower(tails)
        else:
            heads_u, back_u = right_upper(heads), right_upper(back)
            t = times(heads_u, m)
            g = (1.0 - t[0], -t[1], -t[2], 1.0 - t[3])
            scale = 1.0 / (g[0] * g[3] - g[1] * g[2])
            g = (g[3] * scale, -g[1] * scale, -g[2] * scale, g[0] * scale)
            inner = apply(g, minus(ya, apply(heads_u, p)))
            reach = right_lower(times(g, cross))
            back_um = times(back_u, m)
            p = plus(minus(yb, apply(back_u, p)), apply(back_um, inner))
            m = plus(right_lower(tails), times(back_um, reach))
        steps.append((inner, reach, p, m))
    a = None
    for l in reversed(range(NLINE)):
        inner, reach, _, _ = steps[l]
        zero = ends[0, 0:5, :] * 0.0
        if l == NLINE - 1:
            beta = (zero, zero)
            a = inner
        else:
            beta = (TWO * a[0], ONE * a[0] + TWO * a[1])
            a = minus(inner, apply(reach, a))
        if l == 0:
            alpha = (zero, zero)
        else:
            _, _, p, m = steps[l - 1]
            b = minus(p, apply(m, a))
            alpha = (TWO * b[0] + ONE * b[1], TWO * b[1])
        for m, value in enumerate(alpha + beta):
            forces[l, 5 * m : 5 * m + 5, :] = value


def step_kernel(
    base, frac, cell, live, axial_hbm, sound_hbm, crossing_hbm, state, out,
    base_here, frac_here, cell_here, axial, sound, crossing, full, tables, hots, packed, inbox, cross_out, cross_in, line_in, rows_out, rows_in,
    cells, edges, before_raw, after_raw, before, after, crosses_by, values, lists,
    lead, tail, first, second, inverse, corners, corners_in, wide, narrow, high_part, low_part,
    eliminated, ends, ends_in, forces, forces_in, result,
    load, ask_send, ask_recv, fixed_send, fixed_recv, corner_send, corner_recv, value_send, value_recv,
    row_send, row_recv, trade_send, trade_recv, store,
):
    me, peers = around("cross")
    row, others = around("line")
    down, up = others[0], others[-1]
    rightward, leftward = peers[0], peers[-1]

    loads = []
    for source, target in (
        (base, base_here),
        (frac, frac_here),
        (cell, cell_here),
        (state, full.at[:, pl.ds(2, CL)]),
        (axial_hbm, axial.at[pl.ds(1, CL)]),
        (sound_hbm, sound.at[pl.ds(1, CL)]),
        (crossing_hbm, crossing),
    ):
        loads.append(pltpu.make_async_copy(source, target, load.at[len(loads)]))
        loads[-1].start()
    barrier = pltpu.get_barrier_semaphore()
    partners = [(row, p) for p in peers] + [(r, me) for r in others]
    for device in partners:
        pl.semaphore_signal(barrier, inc=1, device_id=device, device_id_type=MESH)

    for copy in loads[:3]:
        copy.wait()
    for half in range(2):
        lanes = pl.ds(half * 128, 128)
        packed[:, half, :] = base_here[:, lanes].astype(F32)
        for q in range(3):
            packed[:, 2 * q + 2 + half, :] = frac_here[q, :, lanes]
    inbox[me] = packed[me]
    slot = lax.broadcasted_iota(jnp.int32, (1, CAP), 1)
    for p in range(NCROSS):
        cells[0, p : p + 1, :] = jnp.where(slot < live[p], cell_here[p : p + 1, :], -1)

    pl.semaphore_wait(barrier, len(partners))
    for d, p in enumerate(peers):
        remote(packed.at[p], inbox.at[me], ask_send, ask_recv.at[d], (row, p))
    fixed = []

    def fix(source, target, device):
        m = len(fixed)
        fixed.append(remote(source, target, fixed_send.at[m], fixed_recv.at[m], device))

    fix(cells.at[0], cells.at[2], (row, leftward))
    fix(cells.at[0], cells.at[1], (row, rightward))
    for copy in loads[3:]:
        copy.wait()
    fix(axial.at[1], line_in.at[2], (up, me))
    fix(sound.at[1], line_in.at[3], (up, me))
    fix(axial.at[CL], line_in.at[0], (down, me))
    fix(sound.at[CL], line_in.at[1], (down, me))
    cross_out[0] = crossing[:, 0, :]
    cross_out[1] = crossing[:, CJ - 1, :]
    fix(cross_out.at[0], cross_in.at[1], (row, leftward))
    fix(cross_out.at[1], cross_in.at[0], (row, rightward))

    @pl.loop(0, NV)
    def _(v):
        for j in range(2):
            edges[0, v, j] = full[v, pl.ds(2, CL), j, :]
            edges[1, v, j] = full[v, pl.ds(2, CL), CJ - 2 + j, :]

    fix(edges.at[0], after_raw, (row, leftward))
    fix(edges.at[1], before_raw, (row, rightward))

    build_tables(full, tables)
    build_hots(inbox[me], hots, 0)

    @pl.loop(0, NCROSS // 2)
    def _(h):
        for k in range(2):
            d = 2 * h + k
            p = lax.rem(me + d, NCROSS)
            ahead = lax.rem(me + d + 1, NCROSS)

            @pl.when(d < 15)
            def _():
                pltpu.make_async_remote_copy(
                    src_ref=packed.at[ahead], dst_ref=inbox.at[ahead], send_sem=ask_send,
                    recv_sem=ask_recv.at[14 - d], device_id=(row, ahead), device_id_type=MESH,
                ).wait_recv()

            build_hots(inbox[ahead], hots, 1 - k)
            answer = donor_products(inbox[p], tables, hots, k)
            values[p] = answer

            @pl.when(d == 0)
            def _():
                lists[0, me] = answer

            @pl.when(d > 0)
            def _():
                remote(values.at[p], lists.at[0, me], value_send.at[0], value_recv.at[0], (row, p))

            @pl.when(d == 15)
            def _():
                lists[1, me] = answer

            @pl.when(d != 15)
            def _():
                remote(values.at[p], lists.at[1, me], value_send.at[1], value_recv.at[1], (row, lax.rem(p + 1, NCROSS)))

            @pl.when(d == 1)
            def _():
                lists[2, me] = answer

            @pl.when(d != 1)
            def _():
                remote(values.at[p], lists.at[2, me], value_send.at[2], value_recv.at[2], (row, lax.rem(p + 15, NCROSS)))

    corners[...] = jnp.zeros(corners.shape, F32)
    for half in range(2):
        elimination(axial, sound, lead, tail, first, second, inverse, corners, half)
    shared = [
        remote(corners.at[r], corners_in.at[row], corner_send.at[d], corner_recv.at[d], (r, me))
        for d, r in enumerate(others)
    ]
    corners_in[row] = corners[row]

    most = pl.ds(0, 15)
    pltpu.make_async_remote_copy(
        src_ref=packed.at[most], dst_ref=inbox.at[most], send_sem=ask_send, recv_sem=ask_recv.at[0],
        device_id=(row, rightward), device_id_type=MESH,
    ).wait_send()
    for m in range(3):
        pltpu.make_async_remote_copy(
            src_ref=values.at[most], dst_ref=lists.at[m, most], send_sem=value_send.at[m], recv_sem=value_recv.at[m],
            device_id=(row, rightward), device_id_type=MESH,
        ).wait()
    for copy in fixed:
        copy.wait()
    axial[0], sound[0], axial[CL + 1], sound[CL + 1] = line_in[0], line_in[1], line_in[2], line_in[3]

    def inside(flag, value):
        return jnp.where(flag, value, 0.0)

    build_depths(cells, 0, wide, narrow)

    @pl.loop(0, 4)
    def _(n):
        t = lax.rem(n * 3, 4)
        rows = lax.broadcasted_iota(jnp.int32, (128, CAP), 0) + t * 128
        taken, fresh = place_values(lists, cells, 0, rows, wide, narrow, high_part, low_part)
        span = pl.ds(2 + t * 16, 16)
        for v in range(NV):
            full[v, span] = jnp.where(taken, fresh[v], full[v, span].reshape(128, NK)).reshape(16, CJ, NK)

        @pl.when(n == 1)
        def _():
            rows_out[0] = full[:, pl.ds(2, 2)]
            rows_out[1] = full[:, pl.ds(CL, 2)]
            remote(rows_out.at[0], rows_in.at[1], row_send.at[0], row_recv.at[0], (up, me))
            remote(rows_out.at[1], rows_in.at[0], row_send.at[1], row_recv.at[1], (down, me))

    for m, column, raw, target, flag in (
        (1, CJ - 2, before_raw, before, me > 0),
        (2, 0, after_raw, after, me < NCROSS - 1),
    ):
        build_depths(cells, m, wide, narrow)
        order = lax.broadcasted_iota(jnp.int32, (128, CAP), 0)
        rows = lax.bitwise_and(order, 63) * CJ + column + lax.shift_right_logical(order, 6)
        taken, fresh = place_values(lists, cells, m, rows, wide, narrow, high_part, low_part)
        for v in range(NV):
            now = inside(flag, jnp.where(taken, fresh[v], raw[v].reshape(128, NK)))
            for j in range(2):
                for half in range(2):
                    target[half, v, j] = now[j * CL : (j + 1) * CL, half * 128 : half * 128 + 128]
    for half in range(2):
        crosses_by[half] = cross_in[:, :, pl.ds(half * 128, 128)]

    for m, device in enumerate((up, down)):
        pltpu.make_async_remote_copy(
            src_ref=rows_out.at[m], dst_ref=rows_in.at[1 - m], send_sem=row_send.at[m], recv_sem=row_recv.at[m],
            device_id=(device, me), device_id_type=MESH,
        ).wait()
    full[:, pl.ds(0, 2)] = inside(row > 0, rows_in[0])
    full[:, pl.ds(CL + 2, 2)] = inside(row < NLINE - 1, rows_in[1])

    ends[...] = jnp.zeros(ends.shape, F32)
    column = lax.broadcasted_iota(jnp.int32, (CJ, 128), 0)
    for half in range(2):
        lanes = pl.ds(half * 128, 128)
        zero = sound[1, :, lanes] * 0.0

        def eliminate(i, carried):
            speed, wave, crosses = axial[i + 1, :, lanes], sound[i + 1, :, lanes], crossing[i, :, lanes]
            rho = jnp.abs(speed) + wave
            speed_up, wave_up = axial[i, :, lanes], sound[i, :, lanes]
            speed_down, wave_down = axial[i + 2, :, lanes], sound[i + 2, :, lanes]
            here = pl.ds(i, 1)
            cross_left = jnp.where(column == 0, crosses_by[half, 0, here, :], pltpu.roll(crosses, 1, 0))
            cross_right = jnp.where(column == CJ - 1, crosses_by[half, 1, here, :], pltpu.roll(crosses, CJ - 1, 0))
            following = []
            for v in range(NV):
                s = SETS[v]
                y1, y2, low, high = carried[v]
                q = full[v, i + 2, :, lanes]
                above, below = full[v, i + 1, :, lanes], full[v, i + 3, :, lanes]
                fourth = full[v, i, :, lanes] + full[v, i + 4, :, lanes] - 4.0 * (above + below) + 6.0 * q
                l2, l1 = before[half, v, 0, here, :], before[half, v, 1, here, :]
                r1, r2 = after[half, v, 0, here, :], after[half, v, 1, here, :]
                left1 = jnp.where(column == 0, l1, pltpu.roll(q, 1, 0))
                left2 = jnp.where(column == 0, l2, jnp.where(column == 1, l1, pltpu.roll(q, 2, 0)))
                right1 = jnp.where(column == CJ - 1, r1, pltpu.roll(q, CJ - 1, 0))
                right2 = jnp.where(column == CJ - 1, r2, jnp.where(column == CJ - 2, r1, pltpu.roll(q, CJ - 2, 0)))
                fourth_cross = left2 + right2 - 4.0 * (left1 + right1) + 6.0 * q
                source = (
                    -4.0 * ((speed_down + SIGMA[s] * wave_down) * below - (speed_up + SIGMA[s] * wave_up) * above)
                    - 4.0 * (cross_right * right1 - cross_left * left1)
                    - 8.0 * rho * (fourth + 0.03125 * fourth_cross)
                )
                p1 = lead[s, jnp.maximum(i - 1, 0), :, lanes]
                q2 = tail[s, jnp.maximum(i - 2, 0), :, lanes]
                y = source * inverse[s, i, :, lanes] - p1 * y1 - q2 * y2
                eliminated[v, i, :, lanes] = y
                t = y * (0.5 * tail[s, i, :, lanes])
                following.append((y, y1, low + first[s, i, :, lanes] * t, high + second[s, i, :, lanes] * t))
            return tuple(following)

        done = lax.fori_loop(0, CL, eliminate, (((zero,) * 4),) * NV, unroll=2)
        for v in range(NV):
            s = SETS[v]
            y1, y2, low, high = done[v]
            last = 0.5 * tail[s, CL - 1, :, lanes] * y1
            ends[:, v, lanes] = low
            ends[:, 5 + v, lanes] = high
            ends[:, 10 + v, lanes] = 0.5 * tail[s, CL - 2, :, lanes] * y2 - lead[s, CL - 2, :, lanes] * last
            ends[:, 15 + v, lanes] = last

    def trade(source, target, m):
        copies = [
            remote(source.at[r], target.at[row], trade_send.at[m, d], trade_recv.at[m, d], (r, me))
            for d, r in enumerate(others)
        ]
        target[row] = source[row]
        return copies

    sent = trade(ends, ends_in, 0)
    for copy in shared + sent:
        copy.wait()
    solve_interface(ends_in, corners_in, forces)
    for copy in trade(forces, forces_in, 1):
        copy.wait()

    both = [(v, half, pl.ds(half * 128, 128)) for half in range(2) for v in range(NV)]

    def forced(v, i, lanes):
        s = SETS[v]
        alpha0, alpha1 = forces_in[:, v, lanes], forces_in[:, 5 + v, lanes]
        return (
            eliminated[v, i, :, lanes] - first[s, i, :, lanes] * alpha0 - second[s, i, :, lanes] * alpha1
        )

    start = []
    for v, half, lanes in both:
        s = SETS[v]
        beta0, beta1 = forces_in[:, 10 + v, lanes], forces_in[:, 15 + v, lanes]
        p2 = lead[s, CL - 2, :, lanes]
        last = (forced(v, CL - 1, lanes) - beta1 + p2 * beta0) * (0.5 * tail[s, CL - 1, :, lanes])
        prior = (forced(v, CL - 2, lanes) - beta0) * (0.5 * tail[s, CL - 2, :, lanes]) - p2 * last
        result[3, v, 15, :, lanes] = full[v, CL + 1, :, lanes] + last
        result[3, v, 14, :, lanes] = full[v, CL, :, lanes] + prior
        start.append((prior, last))

    def substitute(t, carried):
        i = CL - 3 - t
        following = []
        for (v, half, lanes), (x1, x2) in zip(both, carried):
            s = SETS[v]
            x = (0.5 * forced(v, i, lanes) - x2) * tail[s, i, :, lanes] - lead[s, i, :, lanes] * x1
            result[i // 16, v, i % 16, :, lanes] = full[v, i + 2, :, lanes] + x
            following.append((x, x1))

        @pl.when(lax.rem(i, 16) == 0)
        def _():
            pltpu.make_async_copy(result.at[i // 16], out.at[:, pl.ds(i, 16)], store.at[i // 16]).start()

        return tuple(following)

    lax.fori_loop(0, CL - 2, substitute, tuple(start), unroll=2)
    for n in range(4):
        pltpu.make_async_copy(result.at[n], out.at[:, pl.ds(16 * n, 16)], store.at[n]).wait()


def on_device(
    state, axial_speed, sound_speed, cross_speed, donor_base, donor_frac, fringe_cell, live_count
):
    sems = pltpu.SemaphoreType.DMA
    block = (NV, CL, CJ, NK)
    part = pltpu.VMEM((3, CL, CJ, NK), F32)
    edge = pltpu.VMEM((NV, 2, CL, NK), F32)
    split = pltpu.VMEM((2, NV, 2, CL, 128), F32)
    packs = pltpu.VMEM((NCROSS, 8, 128), F32)
    shares = pltpu.VMEM((NLINE, 24, NK), F32)
    return pl.pallas_call(
        step_kernel,
        out_shape=jax.ShapeDtypeStruct(block, F32),
        in_specs=[HBM_SPEC] * 3 + [SMEM_SPEC] + [HBM_SPEC] * 4,
        out_specs=HBM_SPEC,
        scratch_shapes=[
            pltpu.VMEM((NCROSS, CAP), jnp.int32),
            pltpu.VMEM((3, NCROSS, CAP), F32),
            pltpu.VMEM((NCROSS, CAP), jnp.int32),
            pltpu.VMEM((CL + 2, CJ, NK), F32),
            pltpu.VMEM((CL + 2, CJ, NK), F32),
            pltpu.VMEM((CL, CJ, NK), F32),
            pltpu.VMEM((NV, CL + 4, CJ, NK), F32),
            pltpu.VMEM((4, NV, NK, 256), BF16),
            pltpu.VMEM((2, 4, 256, CAP), BF16),
            packs,
            packs,
            pltpu.VMEM((2, CL, NK), F32),
            pltpu.VMEM((2, CL, NK), F32),
            pltpu.VMEM((4, CJ, NK), F32),
            pltpu.VMEM((2, NV, 2, CJ, NK), F32),
            pltpu.VMEM((2, NV, 2, CJ, NK), F32),
            pltpu.VMEM((3, NCROSS, CAP), jnp.int32),
            pltpu.VMEM((2, NV, 2, CL, NK), F32),
            edge,
            edge,
            split,
            split,
            pltpu.VMEM((2, 2, CL, 128), F32),
            pltpu.VMEM((NCROSS, 8, CAP), F32),
            pltpu.VMEM((3, NCROSS, 8, CAP), F32),
            part,
            part,
            part,
            part,
            part,
            pltpu.VMEM((CJ, 32, NK), F32),
            pltpu.VMEM((NLINE, 32, NK), F32),
            pltpu.VMEM((NK, NCROSS * CAP), BF16),
            pltpu.VMEM((NK, NCROSS * CAP), F8),
            pltpu.VMEM((NV * 128, NCROSS * CAP), BF16),
            pltpu.VMEM(((NV + 1) * 128, NCROSS * CAP), F8),
            pltpu.VMEM(block, F32),
            shares,
            shares,
            shares,
            shares,
            pltpu.VMEM((4, NV, 16, CJ, NK), F32),
            sems((7,)),
            sems,
            sems((15,)),
            sems((10,)),
            sems((10,)),
            sems((7,)),
            sems((7,)),
            sems((3,)),
            sems((3,)),
            sems((2,)),
            sems((2,)),
            sems((2, 7)),
            sems((2, 7)),
            sems((4,)),
        ],
        compiler_params=pltpu.CompilerParams(collective_id=0, has_side_effects=True, vmem_limit_bytes=LIMIT),
        name="step",
    )(
        donor_base.reshape(NCROSS, CAP),
        donor_frac.reshape(3, NCROSS, CAP),
        fringe_cell.reshape(NCROSS, CAP),
        live_count.reshape(NCROSS),
        axial_speed,
        sound_speed,
        cross_speed,
        state,
    )


def solution(mesh):
    in_specs = (
        P(None, "line", "cross", None),
        P("line", "cross", None),
        P("line", "cross", None),
        P("line", "cross", None),
        P("line", "cross", None, None),
        P("line", "cross", None, None, None),
        P("line", "cross", None, None),
        P("line", "cross", None),
    )
    out_specs = P(None, "line", "cross", None)
    return jax.shard_map(
        on_device, mesh=mesh, in_specs=in_specs, out_specs=out_specs, check_vma=False
    )
```

```python
import jax
import jax.numpy as jnp
from jax import lax
from jax.experimental import pallas as pl
from jax.experimental.pallas import tpu as pltpu
from jax.sharding import PartitionSpec as P

MESH = pl.DeviceIdType.MESH
F32 = jnp.float32
BF16 = jnp.bfloat16
NV, CL, CJ, NK, CAP = 5, 64, 8, 256, 256
NLINE, NCROSS = 8, 16
SETS = (0, 1, 1, 1, 2)
SIGMA = (-1.0, 0.0, 1.0)
ONE, TWO, MID = -264.0, 2.0, 524.0
F8 = jnp.float8_e4m3fn
LIMIT = 56 * 1024 * 1024
TRANSPOSED = (((1,), (1,)), ((), ()))

VMEM_SPEC = pl.BlockSpec(memory_space=pltpu.VMEM)
SMEM_SPEC = pl.BlockSpec(memory_space=pltpu.SMEM)
HBM_SPEC = pl.BlockSpec(memory_space=pltpu.HBM)


def remote(src, dst, send, recv, device):
    copy = pltpu.make_async_remote_copy(
        src_ref=src, dst_ref=dst, send_sem=send, recv_sem=recv, device_id=device, device_id_type=MESH
    )
    copy.start()
    return copy


def around(axis):
    count = {"line": NLINE, "cross": NCROSS}[axis]
    me = lax.axis_index(axis)
    return me, [lax.rem(me + d, count) for d in range(1, count)]


def build_tables(full, tables):
    odd = lax.bitwise_and(lax.broadcasted_iota(jnp.int32, (CL // 2, CJ, NK), 1), 1) == 1

    @pl.loop(0, NV)
    def _(v):
        pairs = full[v, pl.ds(2, CL)].reshape(CL // 2, 2, CJ, NK)
        for a in range(2):
            high = pairs[:, a].astype(BF16).astype(F32)
            low = pairs[:, a] - high
            for b in range(2):
                if b == 0:
                    mixed = jnp.where(odd, pltpu.roll(low, 1, 1), high)
                else:
                    mixed = jnp.where(odd, high, pltpu.roll(low, CJ - 1, 1))
                tables[2 * a + b, v] = mixed.reshape(256, NK).T.astype(BF16)


def read_request(asked):
    def field(q):
        return jnp.concatenate([asked[2 * q : 2 * q + 1, :], asked[2 * q + 1 : 2 * q + 2, :]], 1)

    origin = field(0).astype(jnp.int32)
    row = lax.shift_right_logical(origin, 11)
    column = lax.bitwise_and(lax.shift_right_logical(origin, 8), 7)
    return row, column, lax.bitwise_and(origin, 255), field(1), field(2), field(3)


def build_hots(asked, hots, slot):
    row, column, _, _, _, _ = read_request(asked)
    place = lax.shift_right_logical(lax.broadcasted_iota(jnp.int32, (256, CAP), 0), 1)
    for a in range(2):
        for b in range(2):
            corner = lax.shift_right_logical(row + 1 - a, 1) * 4 + lax.shift_right_logical(column + 1 - b, 1)
            hots[slot, 2 * a + b] = jnp.where(place == corner, 1.0, 0.0).astype(BF16)


def donor_products(asked, tables, hots, slot):
    row, column, depth, fx, fy, fz = read_request(asked)
    even_row = lax.bitwise_and(row, 1) == 0
    even_column = lax.bitwise_and(column, 1) == 0
    gx, gy, gz = 1.0 - fx, 1.0 - fy, 1.0 - fz
    along_x = (jnp.where(even_row, gx, fx), jnp.where(even_row, fx, gx))
    along_y = (jnp.where(even_column, gy, fy), jnp.where(even_column, fy, gy))
    past = lax.broadcasted_iota(jnp.int32, (NK, CAP), 0) - depth
    along_z = jnp.where(past == 0, gz, jnp.where(past == 1, fz, 0.0))
    sums = [0.0] * NV
    for a in range(2):
        for b in range(2):
            weight = along_x[a] * along_y[b]
            rows = tables[2 * a + b].reshape(NV * NK, 256)
            mixed = jnp.dot(rows, hots[slot, 2 * a + b], preferred_element_type=F32)
            for v in range(NV):
                sums[v] += weight * jnp.sum(mixed[v * NK : (v + 1) * NK] * along_z, axis=0, keepdims=True)
    return jnp.concatenate(sums + [jnp.zeros((3, CAP), F32)], 0)


def build_depths(cells, m, wide, narrow):
    for p in range(NCROSS):
        depth = lax.bitwise_and(cells[m, p : p + 1, :], 255)
        hit = jnp.where(lax.broadcasted_iota(jnp.int32, (NK, CAP), 0) == depth, 1.0, 0.0)
        wide[:, p * CAP : (p + 1) * CAP] = hit.astype(BF16)
        narrow[:, p * CAP : (p + 1) * CAP] = hit.astype(F8)


def place_values(values, cells, m, rows, wide, narrow, high_part, low_part):
    count = rows.shape[0]
    peak = jnp.maximum(jnp.max(jnp.abs(values[m]), axis=(0, 1, 2), keepdims=True)[0], 1e-30)
    scale = 65536.0 / peak
    for p in range(NCROSS):
        lanes = slice(p * CAP, (p + 1) * CAP)
        hit = rows == lax.shift_right_arithmetic(cells[m, p : p + 1, :], 8)
        picked = jnp.where(hit, 1.0, 0.0).astype(BF16)
        for v in range(NV):
            here = values[m, p, v : v + 1, :]
            high = here.astype(BF16)
            low = ((here - high.astype(F32)) * scale).astype(BF16)
            high_part[v * count : (v + 1) * count, lanes] = picked * high
            low_part[v * count : (v + 1) * count, lanes] = (picked * low).astype(F8)
        low_part[NV * count : (NV + 1) * count, lanes] = picked.astype(F8)
    high = lax.dot_general(high_part[0 : NV * count], wide[...], TRANSPOSED, preferred_element_type=F32)
    low = lax.dot_general(low_part[0 : (NV + 1) * count], narrow[...], TRANSPOSED, preferred_element_type=F32)
    unscale = peak * (1.0 / 65536.0)
    fresh = [
        high[v * count : (v + 1) * count] + low[v * count : (v + 1) * count] * unscale for v in range(NV)
    ]
    return low[NV * count :] > 0.5, fresh


def factor_rows(axial, sound, lead, tail, first, second, inverse, carry, start, base, lanes):
    state = [[jnp.where(start, 0.0, carry[11 * s + n]) for n in range(11)] for s in range(3)]
    for k in range(8):
        i = base + k
        speed, wave = axial[i + 1, :, lanes], sound[i + 1, :, lanes]
        rho = jnp.abs(speed) + wave
        for s in range(3):
            e1, p1, q1, q2, a1, a2, b1, b2, aa, ab, bb = state[s]
            r = 1.0 / (rho + 0.5 * jnp.abs(speed + SIGMA[s] * wave))
            inv = 1.0 / ((MID + r) - TWO * q2 - e1 * p1)
            e = ONE - TWO * p1
            p = e * inv
            q = TWO * inv
            a = 0.0 - p1 * a1 - q2 * a2
            b = 0.0 - p1 * b1 - q2 * b2
            if k == 0:
                a = jnp.where(start, 1.0, a)
            if k == 1:
                b = jnp.where(start, 1.0, b)
            ai, bi = a * inv, b * inv
            lead[s, i, :, lanes], tail[s, i, :, lanes] = p, q
            first[s, i, :, lanes], second[s, i, :, lanes], inverse[s, i, :, lanes] = a, b, r
            state[s] = [e, p, q, q1, a, a1, b, b1, aa + ai * a, ab + ai * b, bb + bi * b]
    for s in range(3):
        for n in range(11):
            carry[11 * s + n] = state[s][n]


def inverse_corners(lead, carry, corners, half):
    lanes = pl.ds(half * 128, 128)
    for s in range(3):
        _, _, q1, q2, a1, a2, b1, b2, aa, ab, bb = [carry[11 * s + n] for n in range(11)]
        inv1, inv2, p2 = 0.5 * q1, 0.5 * q2, lead[s, CL - 2, :, lanes]
        entries = (
            aa,
            ab,
            bb,
            a2 * inv2 - a1 * p2 * inv1,
            a1 * inv1,
            b2 * inv2 - b1 * p2 * inv1,
            b1 * inv1,
            inv2 + p2 * p2 * inv1,
            -p2 * inv1,
            inv1,
        )
        for m, entry in enumerate(entries):
            corners[:, 3 * m + s, lanes] = entry


def times(m, n):
    a, b, c, d = m
    e, f, g, h = n
    return (a * e + b * g, a * f + b * h, c * e + d * g, c * f + d * h)


def apply(m, x):
    return (m[0] * x[0] + m[1] * x[1], m[2] * x[0] + m[3] * x[1])


def right_upper(m):
    return (TWO * m[0], ONE * m[0] + TWO * m[1], TWO * m[2], ONE * m[2] + TWO * m[3])


def right_lower(m):
    return (TWO * m[0] + ONE * m[1], TWO * m[1], TWO * m[2] + ONE * m[3], TWO * m[3])


def plus(m, n):
    return tuple(a + b for a, b in zip(m, n))


def minus(m, n):
    return tuple(a - b for a, b in zip(m, n))


def solve_interface(ends, corners, forces, half):
    lanes = slice(half * 128, half * 128 + 128)
    variable = lax.broadcasted_iota(jnp.int32, (NV, 128), 0)

    def corner(l, m):
        rows = [corners[l, 3 * m + s : 3 * m + s + 1, lanes] for s in range(3)]
        return jnp.where(variable == 0, rows[0], jnp.where(variable == 4, rows[2], rows[1]))

    steps = []
    p = m = None
    for l in range(NLINE):
        c = [corner(l, k) for k in range(10)]
        heads = (c[0], c[1], c[1], c[2])
        cross = (c[3], c[4], c[5], c[6])
        back = (c[3], c[5], c[4], c[6])
        tails = (c[7], c[8], c[8], c[9])
        ya = (ends[l, 0:5, :], ends[l, 5:10, :])
        yb = (ends[l, 10:15, :], ends[l, 15:20, :])
        if l == 0:
            inner, reach = ya, right_lower(cross)
            p, m = yb, right_lower(tails)
        else:
            heads_u, back_u = right_upper(heads), right_upper(back)
            t = times(heads_u, m)
            g = (1.0 - t[0], -t[1], -t[2], 1.0 - t[3])
            scale = 1.0 / (g[0] * g[3] - g[1] * g[2])
            g = (g[3] * scale, -g[1] * scale, -g[2] * scale, g[0] * scale)
            inner = apply(g, minus(ya, apply(heads_u, p)))
            reach = right_lower(times(g, cross))
            back_um = times(back_u, m)
            p = plus(minus(yb, apply(back_u, p)), apply(back_um, inner))
            m = plus(right_lower(tails), times(back_um, reach))
        steps.append((inner, reach, p, m))
    a = None
    for l in reversed(range(NLINE)):
        inner, reach, _, _ = steps[l]
        zero = ends[0, 0:5, :] * 0.0
        if l == NLINE - 1:
            beta = (zero, zero)
            a = inner
        else:
            beta = (TWO * a[0], ONE * a[0] + TWO * a[1])
            a = minus(inner, apply(reach, a))
        if l == 0:
            alpha = (zero, zero)
        else:
            _, _, p, m = steps[l - 1]
            b = minus(p, apply(m, a))
            alpha = (TWO * b[0] + ONE * b[1], TWO * b[1])
        for m, value in enumerate(alpha + beta):
            forces[l, 5 * m : 5 * m + 5, :] = value


def step_kernel(
    base, frac, cell, live, axial_hbm, sound_hbm, crossing_hbm, state, out,
    base_here, frac_here, cell_here, axial, sound, crossing, full, tables, hots, packed, inbox, cross_out, cross_in, line_in, rows_out, rows_in,
    cells, edges, before_raw, after_raw, before, after, crosses_by, values, lists,
    lead, tail, first, second, inverse, carry, corners, corners_in, wide, narrow, high_part, low_part,
    eliminated, ends, ends_in, forces, forces_in,
    load, ask_send, ask_recv, fixed_send, fixed_recv, corner_send, corner_recv, value_send, value_recv,
    row_send, row_recv, edge_send, edge_recv, trade_send, trade_recv,
):
    me, peers = around("cross")
    row, others = around("line")
    down, up = others[0], others[-1]
    rightward, leftward = peers[0], peers[-1]

    loads = []
    for source, target in (
        (base, base_here),
        (frac, frac_here),
        (cell, cell_here),
        (state, full.at[:, pl.ds(2, CL)]),
        (axial_hbm, axial.at[pl.ds(1, CL)]),
        (sound_hbm, sound.at[pl.ds(1, CL)]),
        (crossing_hbm, crossing),
    ):
        loads.append(pltpu.make_async_copy(source, target, load.at[len(loads)]))
        loads[-1].start()
    barrier = pltpu.get_barrier_semaphore()
    partners = [(row, p) for p in peers] + [(r, me) for r in others]
    for device in partners:
        pl.semaphore_signal(barrier, inc=1, device_id=device, device_id_type=MESH)

    for copy in loads[:3]:
        copy.wait()
    for half in range(2):
        lanes = pl.ds(half * 128, 128)
        packed[:, half, :] = base_here[:, lanes].astype(F32)
        for q in range(3):
            packed[:, 2 * q + 2 + half, :] = frac_here[q, :, lanes]
    inbox[me] = packed[me]
    slot = lax.broadcasted_iota(jnp.int32, (1, CAP), 1)
    for p in range(NCROSS):
        cells[0, p : p + 1, :] = jnp.where(slot < live[p], cell_here[p : p + 1, :], -1)

    for copy in loads[3:]:
        copy.wait()
    cross_out[0] = crossing[:, 0, :]
    cross_out[1] = crossing[:, CJ - 1, :]

    @pl.loop(0, NV)
    def _(v):
        for j in range(2):
            edges[0, v, j] = full[v, pl.ds(2, CL), j, :]
            edges[1, v, j] = full[v, pl.ds(2, CL), CJ - 2 + j, :]

    pl.semaphore_wait(barrier, len(partners))
    for d, p in enumerate(peers):
        remote(packed.at[p], inbox.at[me], ask_send, ask_recv.at[d], (row, p))
    fixed = []

    def fix(source, target, device):
        m = len(fixed)
        fixed.append(remote(source, target, fixed_send.at[m], fixed_recv.at[m], device))

    fix(cells.at[0], cells.at[2], (row, leftward))
    fix(cells.at[0], cells.at[1], (row, rightward))
    fix(axial.at[1], line_in.at[2], (up, me))
    fix(sound.at[1], line_in.at[3], (up, me))
    fix(axial.at[CL], line_in.at[0], (down, me))
    fix(sound.at[CL], line_in.at[1], (down, me))
    fix(cross_out.at[0], cross_in.at[1], (row, leftward))
    fix(cross_out.at[1], cross_in.at[0], (row, rightward))

    def send_edge(side, v, j):
        target, device = ((after_raw, (row, leftward)), (before_raw, (row, rightward)))[side]
        remote(edges.at[side, v, j], target.at[v, j], edge_send.at[side], edge_recv.at[side], device)

    build_tables(full, tables)
    build_hots(inbox[me], hots, 0)
    corners[...] = jnp.zeros(corners.shape, F32)

    @pl.loop(0, NCROSS // 2)
    def _(h):
        for k in range(2):
            d = 2 * h + k
            p = lax.rem(me + d, NCROSS)
            ahead = lax.rem(me + d + 1, NCROSS)

            @pl.when(d < 15)
            def _():
                pltpu.make_async_remote_copy(
                    src_ref=packed.at[ahead], dst_ref=inbox.at[ahead], send_sem=ask_send,
                    recv_sem=ask_recv.at[14 - d], device_id=(row, ahead), device_id_type=MESH,
                ).wait_recv()

            build_hots(inbox[ahead], hots, 1 - k)
            answer = donor_products(inbox[p], tables, hots, k)
            values[p] = answer
            send_edge(k, h // 2, h % 2)
            lanes = pl.ds(pl.multiple_of((h // 4) * 128, 128), 128)
            start = d % 8 == 0
            factor_rows(axial, sound, lead, tail, first, second, inverse, carry, start, (d % 8) * 8, lanes)
            for half in range(2):

                @pl.when(d == 8 * half + 7)
                def _():
                    inverse_corners(lead, carry, corners, half)

            @pl.when(d == 0)
            def _():
                lists[0, me] = answer

            @pl.when(d > 0)
            def _():
                remote(values.at[p], lists.at[0, me], value_send.at[0], value_recv.at[0], (row, p))

            @pl.when(d == 15)
            def _():
                lists[1, me] = answer

            @pl.when(d != 15)
            def _():
                remote(values.at[p], lists.at[1, me], value_send.at[1], value_recv.at[1], (row, lax.rem(p + 1, NCROSS)))

            @pl.when(d == 1)
            def _():
                lists[2, me] = answer

            @pl.when(d != 1)
            def _():
                remote(values.at[p], lists.at[2, me], value_send.at[2], value_recv.at[2], (row, lax.rem(p + 15, NCROSS)))

    for side in range(2):
        for j in range(2):
            send_edge(side, NV - 1, j)
    shared = [
        remote(corners.at[r], corners_in.at[row], corner_send.at[d], corner_recv.at[d], (r, me))
        for d, r in enumerate(others)
    ]
    corners_in[row] = corners[row]
    for copy in fixed:
        copy.wait()
    axial[0], sound[0], axial[CL + 1], sound[CL + 1] = line_in[0], line_in[1], line_in[2], line_in[3]
    for half in range(2):
        crosses_by[half] = cross_in[:, :, pl.ds(half * 128, 128)]
    for m in range(3):
        build_depths(cells, m, wide.at[m], narrow.at[m])

    most = pl.ds(0, 15)
    pltpu.make_async_remote_copy(
        src_ref=packed.at[most], dst_ref=inbox.at[most], send_sem=ask_send, recv_sem=ask_recv.at[0],
        device_id=(row, rightward), device_id_type=MESH,
    ).wait_send()
    for m in range(3):
        pltpu.make_async_remote_copy(
            src_ref=values.at[most], dst_ref=lists.at[m, most], send_sem=value_send.at[m], recv_sem=value_recv.at[m],
            device_id=(row, rightward), device_id_type=MESH,
        ).wait()
    def inside(flag, value):
        return jnp.where(flag, value, 0.0)

    @pl.loop(0, 4)
    def _(n):
        t = (3 * n) % 4
        rows = lax.broadcasted_iota(jnp.int32, (128, CAP), 0) + t * 128
        taken, fresh = place_values(lists, cells, 0, rows, wide.at[0], narrow.at[0], high_part, low_part)
        span = pl.ds(2 + t * 16, 16)
        for v in range(NV):
            full[v, span] = jnp.where(taken, fresh[v], full[v, span].reshape(128, NK)).reshape(16, CJ, NK)

        @pl.when(n == 1)
        def _():
            rows_out[0] = full[:, pl.ds(2, 2)]
            rows_out[1] = full[:, pl.ds(CL, 2)]
            remote(rows_out.at[0], rows_in.at[1], row_send.at[0], row_recv.at[0], (up, me))
            remote(rows_out.at[1], rows_in.at[0], row_send.at[1], row_recv.at[1], (down, me))

    for side, raw in enumerate((after_raw, before_raw)):
        pltpu.make_async_remote_copy(
            src_ref=edges.at[side], dst_ref=raw, send_sem=edge_send.at[side], recv_sem=edge_recv.at[side],
            device_id=(row, (leftward, rightward)[side]), device_id_type=MESH,
        ).wait()
    for m, column, raw, target, flag in (
        (1, CJ - 2, before_raw, before, me > 0),
        (2, 0, after_raw, after, me < NCROSS - 1),
    ):
        order = lax.broadcasted_iota(jnp.int32, (128, CAP), 0)
        rows = lax.bitwise_and(order, 63) * CJ + column + lax.shift_right_logical(order, 6)
        taken, fresh = place_values(lists, cells, m, rows, wide.at[m], narrow.at[m], high_part, low_part)
        for v in range(NV):
            now = inside(flag, jnp.where(taken, fresh[v], raw[v].reshape(128, NK)))
            for j in range(2):
                for half in range(2):
                    target[half, v, j] = now[j * CL : (j + 1) * CL, half * 128 : half * 128 + 128]
    for m, device in enumerate((up, down)):
        pltpu.make_async_remote_copy(
            src_ref=rows_out.at[m], dst_ref=rows_in.at[1 - m], send_sem=row_send.at[m], recv_sem=row_recv.at[m],
            device_id=(device, me), device_id_type=MESH,
        ).wait()
    full[:, pl.ds(0, 2)] = inside(row > 0, rows_in[0])
    full[:, pl.ds(CL + 2, 2)] = inside(row < NLINE - 1, rows_in[1])

    ends[...] = jnp.zeros(ends.shape, F32)
    column = lax.broadcasted_iota(jnp.int32, (CJ, 128), 0)

    def eliminate(half):
        lanes = pl.ds(half * 128, 128)
        zero = sound[1, :, lanes] * 0.0

        def body(i, carried):
            speed, wave, crosses = axial[i + 1, :, lanes], sound[i + 1, :, lanes], crossing[i, :, lanes]
            rho = jnp.abs(speed) + wave
            speed_up, wave_up = axial[i, :, lanes], sound[i, :, lanes]
            speed_down, wave_down = axial[i + 2, :, lanes], sound[i + 2, :, lanes]
            here = pl.ds(i, 1)
            cross_left = jnp.where(column == 0, crosses_by[half, 0, here, :], pltpu.roll(crosses, 1, 0))
            cross_right = jnp.where(column == CJ - 1, crosses_by[half, 1, here, :], pltpu.roll(crosses, CJ - 1, 0))
            by_left, by_right = rho + 4.0 * cross_left, rho - 4.0 * cross_right
            rho32, by_two, by_here = 32.0 * rho, 8.0 * rho, 49.5 * rho
            by_above = [rho32 + 4.0 * (speed_up + SIGMA[s] * wave_up) for s in range(3)]
            by_below = [rho32 - 4.0 * (speed_down + SIGMA[s] * wave_down) for s in range(3)]
            following = []
            for v in range(NV):
                s = SETS[v]
                y1, y2, low, high = carried[v]
                q = full[v, i + 2, :, lanes]
                l2, l1 = before[half, v, 0, here, :], before[half, v, 1, here, :]
                r1, r2 = after[half, v, 0, here, :], after[half, v, 1, here, :]
                left1 = jnp.where(column == 0, l1, pltpu.roll(q, 1, 0))
                left2 = jnp.where(column == 0, l2, jnp.where(column == 1, l1, pltpu.roll(q, 2, 0)))
                right1 = jnp.where(column == CJ - 1, r1, pltpu.roll(q, CJ - 1, 0))
                right2 = jnp.where(column == CJ - 1, r2, jnp.where(column == CJ - 2, r1, pltpu.roll(q, CJ - 2, 0)))
                two = (full[v, i, :, lanes] + full[v, i + 4, :, lanes]) + 0.03125 * (left2 + right2)
                source = (
                    (by_above[s] * full[v, i + 1, :, lanes] + by_below[s] * full[v, i + 3, :, lanes])
                    + (by_left * left1 + by_right * right1)
                    - (by_two * two + by_here * q)
                )
                p1 = lead[s, jnp.maximum(i - 1, 0), :, lanes]
                q2 = tail[s, jnp.maximum(i - 2, 0), :, lanes]
                y = (source * inverse[s, i, :, lanes] - q2 * y2) - p1 * y1
                eliminated[v, i, :, lanes] = y
                t = y * (0.5 * tail[s, i, :, lanes])
                following.append((y, y1, low + first[s, i, :, lanes] * t, high + second[s, i, :, lanes] * t))
            return tuple(following)

        done = lax.fori_loop(0, CL, body, (((zero,) * 4),) * NV, unroll=2)
        for v in range(NV):
            s = SETS[v]
            y1, y2, low, high = done[v]
            last = 0.5 * tail[s, CL - 1, :, lanes] * y1
            ends[half, :, v, :] = low
            ends[half, :, 5 + v, :] = high
            ends[half, :, 10 + v, :] = 0.5 * tail[s, CL - 2, :, lanes] * y2 - lead[s, CL - 2, :, lanes] * last
            ends[half, :, 15 + v, :] = last

    def trade(source, target, m):
        copies = [
            remote(source.at[r], target.at[row], trade_send.at[m, d], trade_recv.at[m, d], (r, me))
            for d, r in enumerate(others)
        ]
        target[row] = source[row]
        return copies

    def settle(copies):
        for copy in copies:
            copy.wait()

    def substitute(half):
        lanes = pl.ds(half * 128, 128)

        def forced(v, i):
            s = SETS[v]
            alpha0, alpha1 = forces_in[half, :, v, :], forces_in[half, :, 5 + v, :]
            return eliminated[v, i, :, lanes] - first[s, i, :, lanes] * alpha0 - second[s, i, :, lanes] * alpha1

        start = []
        for v in range(NV):
            s = SETS[v]
            beta0, beta1 = forces_in[half, :, 10 + v, :], forces_in[half, :, 15 + v, :]
            p2 = lead[s, CL - 2, :, lanes]
            last = (forced(v, CL - 1) - beta1 + p2 * beta0) * (0.5 * tail[s, CL - 1, :, lanes])
            prior = (forced(v, CL - 2) - beta0) * (0.5 * tail[s, CL - 2, :, lanes]) - p2 * last
            out[v, CL - 1, :, lanes] = full[v, CL + 1, :, lanes] + last
            out[v, CL - 2, :, lanes] = full[v, CL, :, lanes] + prior
            start.append((prior, last))

        def body(t, carried):
            i = CL - 3 - t
            following = []
            for v in range(NV):
                s = SETS[v]
                x1, x2 = carried[v]
                x = (0.5 * forced(v, i) - x2) * tail[s, i, :, lanes] - lead[s, i, :, lanes] * x1
                out[v, i, :, lanes] = full[v, i + 2, :, lanes] + x
                following.append((x, x1))
            return tuple(following)

        lax.fori_loop(0, CL - 2, body, tuple(start), unroll=2)

    eliminate(0)
    first_ends = trade(ends.at[0], ends_in.at[0], 0)
    eliminate(1)
    second_ends = trade(ends.at[1], ends_in.at[1], 1)
    settle(shared + first_ends)
    solve_interface(ends_in.at[0], corners_in, forces.at[0], 0)
    first_forces = trade(forces.at[0], forces_in.at[0], 2)
    settle(second_ends)
    solve_interface(ends_in.at[1], corners_in, forces.at[1], 1)
    second_forces = trade(forces.at[1], forces_in.at[1], 3)
    settle(first_forces)
    substitute(0)
    settle(second_forces)
    substitute(1)


def on_device(
    state, axial_speed, sound_speed, cross_speed, donor_base, donor_frac, fringe_cell, live_count
):
    sems = pltpu.SemaphoreType.DMA
    block = (NV, CL, CJ, NK)
    part = pltpu.VMEM((3, CL, CJ, NK), F32)
    edge = pltpu.VMEM((NV, 2, CL, NK), F32)
    split = pltpu.VMEM((2, NV, 2, CL, 128), F32)
    packs = pltpu.VMEM((NCROSS, 8, 128), F32)
    shares = pltpu.VMEM((2, NLINE, 24, 128), F32)
    return pl.pallas_call(
        step_kernel,
        out_shape=jax.ShapeDtypeStruct(block, F32),
        in_specs=[HBM_SPEC] * 3 + [SMEM_SPEC] + [HBM_SPEC] * 4,
        out_specs=VMEM_SPEC,
        scratch_shapes=[
            pltpu.VMEM((NCROSS, CAP), jnp.int32),
            pltpu.VMEM((3, NCROSS, CAP), F32),
            pltpu.VMEM((NCROSS, CAP), jnp.int32),
            pltpu.VMEM((CL + 2, CJ, NK), F32),
            pltpu.VMEM((CL + 2, CJ, NK), F32),
            pltpu.VMEM((CL, CJ, NK), F32),
            pltpu.VMEM((NV, CL + 4, CJ, NK), F32),
            pltpu.VMEM((4, NV, NK, 256), BF16),
            pltpu.VMEM((2, 4, 256, CAP), BF16),
            packs,
            packs,
            pltpu.VMEM((2, CL, NK), F32),
            pltpu.VMEM((2, CL, NK), F32),
            pltpu.VMEM((4, CJ, NK), F32),
            pltpu.VMEM((2, NV, 2, CJ, NK), F32),
            pltpu.VMEM((2, NV, 2, CJ, NK), F32),
            pltpu.VMEM((3, NCROSS, CAP), jnp.int32),
            pltpu.VMEM((2, NV, 2, CL, NK), F32),
            edge,
            edge,
            split,
            split,
            pltpu.VMEM((2, 2, CL, 128), F32),
            pltpu.VMEM((NCROSS, 8, CAP), F32),
            pltpu.VMEM((3, NCROSS, 8, CAP), F32),
            part,
            part,
            part,
            part,
            part,
            pltpu.VMEM((33, CJ, 128), F32),
            pltpu.VMEM((CJ, 32, NK), F32),
            pltpu.VMEM((NLINE, 32, NK), F32),
            pltpu.VMEM((3, NK, NCROSS * CAP), BF16),
            pltpu.VMEM((3, NK, NCROSS * CAP), F8),
            pltpu.VMEM((NV * 128, NCROSS * CAP), BF16),
            pltpu.VMEM(((NV + 1) * 128, NCROSS * CAP), F8),
            pltpu.VMEM(block, F32),
            shares,
            shares,
            shares,
            shares,
            sems((7,)),
            sems,
            sems((15,)),
            sems((8,)),
            sems((8,)),
            sems((7,)),
            sems((7,)),
            sems((3,)),
            sems((3,)),
            sems((2,)),
            sems((2,)),
            sems((2,)),
            sems((2,)),
            sems((4, 7)),
            sems((4, 7)),
        ],
        compiler_params=pltpu.CompilerParams(collective_id=0, has_side_effects=True, vmem_limit_bytes=LIMIT),
        name="step",
    )(
        donor_base.reshape(NCROSS, CAP),
        donor_frac.reshape(3, NCROSS, CAP),
        fringe_cell.reshape(NCROSS, CAP),
        live_count.reshape(NCROSS),
        axial_speed,
        sound_speed,
        cross_speed,
        state,
    )


def solution(mesh):
    in_specs = (
        P(None, "line", "cross", None),
        P("line", "cross", None),
        P("line", "cross", None),
        P("line", "cross", None),
        P("line", "cross", None, None),
        P("line", "cross", None, None, None),
        P("line", "cross", None, None),
        P("line", "cross", None),
    )
    out_specs = P(None, "line", "cross", None)
    return jax.shard_map(
        on_device, mesh=mesh, in_specs=in_specs, out_specs=out_specs, check_vma=False
    )
```

```python
import jax
import jax.numpy as jnp
from jax import lax
from jax.experimental import pallas as pl
from jax.experimental.pallas import tpu as pltpu
from jax.sharding import PartitionSpec as P

MESH = pl.DeviceIdType.MESH
F32 = jnp.float32
BF16 = jnp.bfloat16
NV, CL, CJ, NK, CAP = 5, 64, 8, 256, 256
NLINE, NCROSS = 8, 16
SETS = (0, 1, 1, 1, 2)
SIGMA = (-1.0, 0.0, 1.0)
ONE, TWO, MID = -264.0, 2.0, 524.0
F8 = jnp.float8_e4m3fn
LIMIT = 56 * 1024 * 1024
TRANSPOSED = (((1,), (1,)), ((), ()))

VMEM_SPEC = pl.BlockSpec(memory_space=pltpu.VMEM)
SMEM_SPEC = pl.BlockSpec(memory_space=pltpu.SMEM)
HBM_SPEC = pl.BlockSpec(memory_space=pltpu.HBM)


def remote(src, dst, send, recv, device):
    copy = pltpu.make_async_remote_copy(
        src_ref=src, dst_ref=dst, send_sem=send, recv_sem=recv, device_id=device, device_id_type=MESH
    )
    copy.start()
    return copy


def around(axis):
    count = {"line": NLINE, "cross": NCROSS}[axis]
    me = lax.axis_index(axis)
    return me, [lax.rem(me + d, count) for d in range(1, count)]


def build_tables(full, tables):
    odd = lax.bitwise_and(lax.broadcasted_iota(jnp.int32, (CL // 2, CJ, NK), 1), 1) == 1

    @pl.loop(0, NV)
    def _(v):
        pairs = full[v, pl.ds(2, CL)].reshape(CL // 2, 2, CJ, NK)
        for a in range(2):
            high = pairs[:, a].astype(BF16).astype(F32)
            low = pairs[:, a] - high
            for b in range(2):
                if b == 0:
                    mixed = jnp.where(odd, pltpu.roll(low, 1, 1), high)
                else:
                    mixed = jnp.where(odd, high, pltpu.roll(low, CJ - 1, 1))
                tables[2 * a + b, v] = mixed.reshape(256, NK).T.astype(BF16)


def read_request(asked):
    def field(q):
        return jnp.concatenate([asked[2 * q : 2 * q + 1, :], asked[2 * q + 1 : 2 * q + 2, :]], 1)

    origin = field(0).astype(jnp.int32)
    row = lax.shift_right_logical(origin, 11)
    column = lax.bitwise_and(lax.shift_right_logical(origin, 8), 7)
    return row, column, lax.bitwise_and(origin, 255), field(1), field(2), field(3)


def build_hots(asked, hots, slot):
    row, column, _, _, _, _ = read_request(asked)
    place = lax.shift_right_logical(lax.broadcasted_iota(jnp.int32, (256, CAP), 0), 1)
    for a in range(2):
        for b in range(2):
            corner = lax.shift_right_logical(row + 1 - a, 1) * 4 + lax.shift_right_logical(column + 1 - b, 1)
            hots[slot, 2 * a + b] = jnp.where(place == corner, 1.0, 0.0).astype(BF16)


def donor_products(asked, tables, hots, slot):
    row, column, depth, fx, fy, fz = read_request(asked)
    even_row = lax.bitwise_and(row, 1) == 0
    even_column = lax.bitwise_and(column, 1) == 0
    gx, gy, gz = 1.0 - fx, 1.0 - fy, 1.0 - fz
    along_x = (jnp.where(even_row, gx, fx), jnp.where(even_row, fx, gx))
    along_y = (jnp.where(even_column, gy, fy), jnp.where(even_column, fy, gy))
    past = lax.broadcasted_iota(jnp.int32, (NK, CAP), 0) - depth
    along_z = jnp.where(past == 0, gz, jnp.where(past == 1, fz, 0.0))
    sums = [0.0] * NV
    for a in range(2):
        for b in range(2):
            weight = along_x[a] * along_y[b]
            rows = tables[2 * a + b].reshape(NV * NK, 256)
            mixed = jnp.dot(rows, hots[slot, 2 * a + b], preferred_element_type=F32)
            for v in range(NV):
                sums[v] += weight * jnp.sum(mixed[v * NK : (v + 1) * NK] * along_z, axis=0, keepdims=True)
    return jnp.concatenate(sums + [jnp.zeros((3, CAP), F32)], 0)


def build_depths(cells, m, wide, narrow):
    for p in range(NCROSS):
        depth = lax.bitwise_and(cells[m, p : p + 1, :], 255)
        hit = jnp.where(lax.broadcasted_iota(jnp.int32, (NK, CAP), 0) == depth, 1.0, 0.0)
        wide[:, p * CAP : (p + 1) * CAP] = hit.astype(BF16)
        narrow[:, p * CAP : (p + 1) * CAP] = hit.astype(F8)


def place_values(values, cells, m, rows, wide, narrow, high_part, low_part):
    count = rows.shape[0]
    peak = jnp.maximum(jnp.max(jnp.abs(values[m]), axis=(0, 1, 2), keepdims=True)[0], 1e-30)
    scale = 65536.0 / peak
    for p in range(NCROSS):
        lanes = slice(p * CAP, (p + 1) * CAP)
        hit = rows == lax.shift_right_arithmetic(cells[m, p : p + 1, :], 8)
        picked = jnp.where(hit, 1.0, 0.0).astype(BF16)
        for v in range(NV):
            here = values[m, p, v : v + 1, :]
            high = here.astype(BF16)
            low = ((here - high.astype(F32)) * scale).astype(BF16)
            high_part[v * count : (v + 1) * count, lanes] = picked * high
            low_part[v * count : (v + 1) * count, lanes] = (picked * low).astype(F8)
        low_part[NV * count : (NV + 1) * count, lanes] = picked.astype(F8)
    high = lax.dot_general(high_part[0 : NV * count], wide[...], TRANSPOSED, preferred_element_type=F32)
    low = lax.dot_general(low_part[0 : (NV + 1) * count], narrow[...], TRANSPOSED, preferred_element_type=F32)
    unscale = peak * (1.0 / 65536.0)
    fresh = [
        high[v * count : (v + 1) * count] + low[v * count : (v + 1) * count] * unscale for v in range(NV)
    ]
    return low[NV * count :] > 0.5, fresh


def factor_rows(axial, sound, lead, tail, first, second, inverse, carry, start, base, lanes):
    state = [[jnp.where(start, 0.0, carry[11 * s + n]) for n in range(11)] for s in range(3)]
    for k in range(8):
        i = base + k
        speed, wave = axial[i + 1, :, lanes], sound[i + 1, :, lanes]
        rho = jnp.abs(speed) + wave
        for s in range(3):
            e1, p1, q1, q2, a1, a2, b1, b2, aa, ab, bb = state[s]
            r = 1.0 / (rho + 0.5 * jnp.abs(speed + SIGMA[s] * wave))
            inv = 1.0 / ((MID + r) - TWO * q2 - e1 * p1)
            e = ONE - TWO * p1
            p = e * inv
            q = TWO * inv
            a = 0.0 - p1 * a1 - q2 * a2
            b = 0.0 - p1 * b1 - q2 * b2
            if k == 0:
                a = jnp.where(start, 1.0, a)
            if k == 1:
                b = jnp.where(start, 1.0, b)
            ai, bi = a * inv, b * inv
            lead[s, i, :, lanes], tail[s, i, :, lanes] = p, q
            first[s, i, :, lanes], second[s, i, :, lanes], inverse[s, i, :, lanes] = a, b, r
            state[s] = [e, p, q, q1, a, a1, b, b1, aa + ai * a, ab + ai * b, bb + bi * b]
    for s in range(3):
        for n in range(11):
            carry[11 * s + n] = state[s][n]


def inverse_corners(lead, carry, corners, half):
    lanes = pl.ds(half * 128, 128)
    for s in range(3):
        _, _, q1, q2, a1, a2, b1, b2, aa, ab, bb = [carry[11 * s + n] for n in range(11)]
        inv1, inv2, p2 = 0.5 * q1, 0.5 * q2, lead[s, CL - 2, :, lanes]
        entries = (
            aa,
            ab,
            bb,
            a2 * inv2 - a1 * p2 * inv1,
            a1 * inv1,
            b2 * inv2 - b1 * p2 * inv1,
            b1 * inv1,
            inv2 + p2 * p2 * inv1,
            -p2 * inv1,
            inv1,
        )
        for m, entry in enumerate(entries):
            corners[:, 3 * m + s, lanes] = entry


def times(m, n):
    a, b, c, d = m
    e, f, g, h = n
    return (a * e + b * g, a * f + b * h, c * e + d * g, c * f + d * h)


def apply(m, x):
    return (m[0] * x[0] + m[1] * x[1], m[2] * x[0] + m[3] * x[1])


def right_upper(m):
    return (TWO * m[0], ONE * m[0] + TWO * m[1], TWO * m[2], ONE * m[2] + TWO * m[3])


def right_lower(m):
    return (TWO * m[0] + ONE * m[1], TWO * m[1], TWO * m[2] + ONE * m[3], TWO * m[3])


def plus(m, n):
    return tuple(a + b for a, b in zip(m, n))


def minus(m, n):
    return tuple(a - b for a, b in zip(m, n))


def solve_interface(ends, corners, forces, half):
    lanes = slice(half * 128, half * 128 + 128)
    variable = lax.broadcasted_iota(jnp.int32, (NV, 128), 0)

    def corner(l, m):
        rows = [corners[l, 3 * m + s : 3 * m + s + 1, lanes] for s in range(3)]
        return jnp.where(variable == 0, rows[0], jnp.where(variable == 4, rows[2], rows[1]))

    steps = []
    p = m = None
    for l in range(NLINE):
        c = [corner(l, k) for k in range(10)]
        heads = (c[0], c[1], c[1], c[2])
        cross = (c[3], c[4], c[5], c[6])
        back = (c[3], c[5], c[4], c[6])
        tails = (c[7], c[8], c[8], c[9])
        ya = (ends[l, 0:5, :], ends[l, 5:10, :])
        yb = (ends[l, 10:15, :], ends[l, 15:20, :])
        if l == 0:
            inner, reach = ya, right_lower(cross)
            p, m = yb, right_lower(tails)
        else:
            heads_u, back_u = right_upper(heads), right_upper(back)
            t = times(heads_u, m)
            g = (1.0 - t[0], -t[1], -t[2], 1.0 - t[3])
            scale = 1.0 / (g[0] * g[3] - g[1] * g[2])
            g = (g[3] * scale, -g[1] * scale, -g[2] * scale, g[0] * scale)
            inner = apply(g, minus(ya, apply(heads_u, p)))
            reach = right_lower(times(g, cross))
            back_um = times(back_u, m)
            p = plus(minus(yb, apply(back_u, p)), apply(back_um, inner))
            m = plus(right_lower(tails), times(back_um, reach))
        steps.append((inner, reach, p, m))
    a = None
    for l in reversed(range(NLINE)):
        inner, reach, _, _ = steps[l]
        zero = ends[0, 0:5, :] * 0.0
        if l == NLINE - 1:
            beta = (zero, zero)
            a = inner
        else:
            beta = (TWO * a[0], ONE * a[0] + TWO * a[1])
            a = minus(inner, apply(reach, a))
        if l == 0:
            alpha = (zero, zero)
        else:
            _, _, p, m = steps[l - 1]
            b = minus(p, apply(m, a))
            alpha = (TWO * b[0] + ONE * b[1], TWO * b[1])
        for m, value in enumerate(alpha + beta):
            forces[l, 5 * m : 5 * m + 5, :] = value


def step_kernel(
    base, frac, cell, live, axial_hbm, sound_hbm, crossing_hbm, state, out,
    base_here, frac_here, cell_here, axial, sound, crossing, full, tables, hots, packed, inbox, cross_out, cross_in, line_in, rows_out, rows_in,
    cells, edges, before_raw, after_raw, before, after, crosses_by, values, lists,
    lead, tail, first, second, inverse, carry, corners, corners_in, wide, narrow, high_part, low_part,
    eliminated, ends, ends_in, forces, forces_in,
    load, ask_send, ask_recv, fixed_send, fixed_recv, corner_send, corner_recv, value_send, value_recv, pass_send, pass_recv,
    row_send, row_recv, edge_send, edge_recv, trade_send, trade_recv,
):
    me, peers = around("cross")
    row, others = around("line")
    down, up = others[0], others[-1]
    rightward, leftward = peers[0], peers[-1]

    loads = []
    for source, target in (
        (base, base_here),
        (frac, frac_here),
        (cell, cell_here),
        (state, full.at[:, pl.ds(2, CL)]),
        (axial_hbm, axial.at[pl.ds(1, CL)]),
        (sound_hbm, sound.at[pl.ds(1, CL)]),
        (crossing_hbm, crossing),
    ):
        loads.append(pltpu.make_async_copy(source, target, load.at[len(loads)]))
        loads[-1].start()
    barrier = pltpu.get_barrier_semaphore()
    partners = [(row, p) for p in peers] + [(r, me) for r in others]
    for device in partners:
        pl.semaphore_signal(barrier, inc=1, device_id=device, device_id_type=MESH)

    for copy in loads[:3]:
        copy.wait()
    for half in range(2):
        lanes = pl.ds(half * 128, 128)
        packed[:, half, :] = base_here[:, lanes].astype(F32)
        for q in range(3):
            packed[:, 2 * q + 2 + half, :] = frac_here[q, :, lanes]
    inbox[me] = packed[me]
    slot = lax.broadcasted_iota(jnp.int32, (1, CAP), 1)
    for p in range(NCROSS):
        cells[0, p : p + 1, :] = jnp.where(slot < live[p], cell_here[p : p + 1, :], -1)

    for copy in loads[3:]:
        copy.wait()
    cross_out[0] = crossing[:, 0, :]
    cross_out[1] = crossing[:, CJ - 1, :]

    @pl.loop(0, NV)
    def _(v):
        for j in range(2):
            edges[0, v, j] = full[v, pl.ds(2, CL), j, :]
            edges[1, v, j] = full[v, pl.ds(2, CL), CJ - 2 + j, :]

    pl.semaphore_wait(barrier, len(partners))
    for d, p in enumerate(peers):
        remote(packed.at[p], inbox.at[me], ask_send, ask_recv.at[d], (row, p))
    fixed = []

    def fix(source, target, device):
        m = len(fixed)
        fixed.append(remote(source, target, fixed_send.at[m], fixed_recv.at[m], device))

    fix(cells.at[0], cells.at[2], (row, leftward))
    fix(cells.at[0], cells.at[1], (row, rightward))
    fix(axial.at[1], line_in.at[2], (up, me))
    fix(sound.at[1], line_in.at[3], (up, me))
    fix(axial.at[CL], line_in.at[0], (down, me))
    fix(sound.at[CL], line_in.at[1], (down, me))
    fix(cross_out.at[0], cross_in.at[1], (row, leftward))
    fix(cross_out.at[1], cross_in.at[0], (row, rightward))

    def send_edge(side, v):
        target, device = ((after_raw, (row, leftward)), (before_raw, (row, rightward)))[side]
        remote(edges.at[side, v], target.at[v], edge_send.at[side], edge_recv.at[side], device)

    build_tables(full, tables)
    build_hots(inbox[me], hots, 0)
    corners[...] = jnp.zeros(corners.shape, F32)

    @pl.loop(0, NCROSS // 2)
    def _(h):
        for k in range(2):
            d = 2 * h + k
            p = lax.rem(me + d, NCROSS)
            ahead = lax.rem(me + d + 1, NCROSS)

            @pl.when(d < 15)
            def _():
                pltpu.make_async_remote_copy(
                    src_ref=packed.at[ahead], dst_ref=inbox.at[ahead], send_sem=ask_send,
                    recv_sem=ask_recv.at[14 - d], device_id=(row, ahead), device_id_type=MESH,
                ).wait_recv()

            build_hots(inbox[ahead], hots, 1 - k)
            answer = donor_products(inbox[p], tables, hots, k)
            values[p] = answer

            @pl.when(h < NV)
            def _():
                send_edge(k, h)

            lanes = pl.ds(pl.multiple_of((h // 4) * 128, 128), 128)
            start = d % 8 == 0
            @pl.when(d == 0)
            def _():
                lists[0, me] = answer

            @pl.when(d > 0)
            def _():
                remote(values.at[p], lists.at[0, me], value_send, value_recv, (row, p))

    for half in range(2):

        @pl.loop(0, 8)
        def _(block):
            lanes = pl.ds(half * 128, 128)
            factor_rows(axial, sound, lead, tail, first, second, inverse, carry, block == 0, block * 8, lanes)

        inverse_corners(lead, carry, corners, half)
    shared = [
        remote(corners.at[r], corners_in.at[row], corner_send.at[d], corner_recv.at[d], (r, me))
        for d, r in enumerate(others)
    ]
    corners_in[row] = corners[row]
    for copy in fixed:
        copy.wait()
    axial[0], sound[0], axial[CL + 1], sound[CL + 1] = line_in[0], line_in[1], line_in[2], line_in[3]
    for half in range(2):
        crosses_by[half] = cross_in[:, :, pl.ds(half * 128, 128)]
    for m in range(3):
        build_depths(cells, m, wide.at[m], narrow.at[m])

    most = pl.ds(0, 15)
    pltpu.make_async_remote_copy(
        src_ref=packed.at[most], dst_ref=inbox.at[most], send_sem=ask_send, recv_sem=ask_recv.at[0],
        device_id=(row, rightward), device_id_type=MESH,
    ).wait_send()
    pltpu.make_async_remote_copy(
        src_ref=values.at[most], dst_ref=lists.at[0, most], send_sem=value_send, recv_sem=value_recv,
        device_id=(row, rightward), device_id_type=MESH,
    ).wait()
    passed = [
        remote(lists.at[0], lists.at[1], pass_send.at[0], pass_recv.at[0], (row, rightward)),
        remote(lists.at[0], lists.at[2], pass_send.at[1], pass_recv.at[1], (row, leftward)),
    ]

    def inside(flag, value):
        return jnp.where(flag, value, 0.0)

    @pl.loop(0, 4)
    def _(n):
        t = (3 * n) % 4
        rows = lax.broadcasted_iota(jnp.int32, (128, CAP), 0) + t * 128
        taken, fresh = place_values(lists, cells, 0, rows, wide.at[0], narrow.at[0], high_part, low_part)
        span = pl.ds(2 + t * 16, 16)
        for v in range(NV):
            full[v, span] = jnp.where(taken, fresh[v], full[v, span].reshape(128, NK)).reshape(16, CJ, NK)

        @pl.when(n == 1)
        def _():
            rows_out[0] = full[:, pl.ds(2, 2)]
            rows_out[1] = full[:, pl.ds(CL, 2)]
            remote(rows_out.at[0], rows_in.at[1], row_send.at[0], row_recv.at[0], (up, me))
            remote(rows_out.at[1], rows_in.at[0], row_send.at[1], row_recv.at[1], (down, me))

    for copy in passed:
        copy.wait()
    for side, raw in enumerate((after_raw, before_raw)):
        pltpu.make_async_remote_copy(
            src_ref=edges.at[side], dst_ref=raw, send_sem=edge_send.at[side], recv_sem=edge_recv.at[side],
            device_id=(row, (leftward, rightward)[side]), device_id_type=MESH,
        ).wait()
    for m, column, raw, target, flag in (
        (1, CJ - 2, before_raw, before, me > 0),
        (2, 0, after_raw, after, me < NCROSS - 1),
    ):
        order = lax.broadcasted_iota(jnp.int32, (128, CAP), 0)
        rows = lax.bitwise_and(order, 63) * CJ + column + lax.shift_right_logical(order, 6)
        taken, fresh = place_values(lists, cells, m, rows, wide.at[m], narrow.at[m], high_part, low_part)
        for v in range(NV):
            now = inside(flag, jnp.where(taken, fresh[v], raw[v].reshape(128, NK)))
            for j in range(2):
                for half in range(2):
                    target[half, v, j] = now[j * CL : (j + 1) * CL, half * 128 : half * 128 + 128]
    for m, device in enumerate((up, down)):
        pltpu.make_async_remote_copy(
            src_ref=rows_out.at[m], dst_ref=rows_in.at[1 - m], send_sem=row_send.at[m], recv_sem=row_recv.at[m],
            device_id=(device, me), device_id_type=MESH,
        ).wait()
    full[:, pl.ds(0, 2)] = inside(row > 0, rows_in[0])
    full[:, pl.ds(CL + 2, 2)] = inside(row < NLINE - 1, rows_in[1])

    ends[...] = jnp.zeros(ends.shape, F32)
    column = lax.broadcasted_iota(jnp.int32, (CJ, 128), 0)

    def eliminate(half):
        lanes = pl.ds(half * 128, 128)
        zero = sound[1, :, lanes] * 0.0

        def body(i, carried):
            speed, wave, crosses = axial[i + 1, :, lanes], sound[i + 1, :, lanes], crossing[i, :, lanes]
            rho = jnp.abs(speed) + wave
            speed_up, wave_up = axial[i, :, lanes], sound[i, :, lanes]
            speed_down, wave_down = axial[i + 2, :, lanes], sound[i + 2, :, lanes]
            here = pl.ds(i, 1)
            cross_left = jnp.where(column == 0, crosses_by[half, 0, here, :], pltpu.roll(crosses, 1, 0))
            cross_right = jnp.where(column == CJ - 1, crosses_by[half, 1, here, :], pltpu.roll(crosses, CJ - 1, 0))
            by_left, by_right = rho + 4.0 * cross_left, rho - 4.0 * cross_right
            rho32, by_two, by_here = 32.0 * rho, 8.0 * rho, 49.5 * rho
            by_above = [rho32 + 4.0 * (speed_up + SIGMA[s] * wave_up) for s in range(3)]
            by_below = [rho32 - 4.0 * (speed_down + SIGMA[s] * wave_down) for s in range(3)]
            following = []
            for v in range(NV):
                s = SETS[v]
                y1, y2, low, high = carried[v]
                q = full[v, i + 2, :, lanes]
                l2, l1 = before[half, v, 0, here, :], before[half, v, 1, here, :]
                r1, r2 = after[half, v, 0, here, :], after[half, v, 1, here, :]
                left1 = jnp.where(column == 0, l1, pltpu.roll(q, 1, 0))
                left2 = jnp.where(column == 0, l2, jnp.where(column == 1, l1, pltpu.roll(q, 2, 0)))
                right1 = jnp.where(column == CJ - 1, r1, pltpu.roll(q, CJ - 1, 0))
                right2 = jnp.where(column == CJ - 1, r2, jnp.where(column == CJ - 2, r1, pltpu.roll(q, CJ - 2, 0)))
                two = (full[v, i, :, lanes] + full[v, i + 4, :, lanes]) + 0.03125 * (left2 + right2)
                source = (
                    (by_above[s] * full[v, i + 1, :, lanes] + by_below[s] * full[v, i + 3, :, lanes])
                    + (by_left * left1 + by_right * right1)
                    - (by_two * two + by_here * q)
                )
                p1 = lead[s, jnp.maximum(i - 1, 0), :, lanes]
                q2 = tail[s, jnp.maximum(i - 2, 0), :, lanes]
                y = (source * inverse[s, i, :, lanes] - q2 * y2) - p1 * y1
                eliminated[v, i, :, lanes] = y
                t = y * (0.5 * tail[s, i, :, lanes])
                following.append((y, y1, low + first[s, i, :, lanes] * t, high + second[s, i, :, lanes] * t))
            return tuple(following)

        done = lax.fori_loop(0, CL, body, (((zero,) * 4),) * NV, unroll=2)
        for v in range(NV):
            s = SETS[v]
            y1, y2, low, high = done[v]
            last = 0.5 * tail[s, CL - 1, :, lanes] * y1
            ends[half, :, v, :] = low
            ends[half, :, 5 + v, :] = high
            ends[half, :, 10 + v, :] = 0.5 * tail[s, CL - 2, :, lanes] * y2 - lead[s, CL - 2, :, lanes] * last
            ends[half, :, 15 + v, :] = last

    def trade(source, target, m):
        copies = [
            remote(source.at[r], target.at[row], trade_send.at[m, d], trade_recv.at[m, d], (r, me))
            for d, r in enumerate(others)
        ]
        target[row] = source[row]
        return copies

    def settle(copies):
        for copy in copies:
            copy.wait()

    def substitute(half):
        lanes = pl.ds(half * 128, 128)

        def forced(v, i):
            s = SETS[v]
            alpha0, alpha1 = forces_in[half, :, v, :], forces_in[half, :, 5 + v, :]
            return eliminated[v, i, :, lanes] - first[s, i, :, lanes] * alpha0 - second[s, i, :, lanes] * alpha1

        start = []
        for v in range(NV):
            s = SETS[v]
            beta0, beta1 = forces_in[half, :, 10 + v, :], forces_in[half, :, 15 + v, :]
            p2 = lead[s, CL - 2, :, lanes]
            last = (forced(v, CL - 1) - beta1 + p2 * beta0) * (0.5 * tail[s, CL - 1, :, lanes])
            prior = (forced(v, CL - 2) - beta0) * (0.5 * tail[s, CL - 2, :, lanes]) - p2 * last
            out[v, CL - 1, :, lanes] = full[v, CL + 1, :, lanes] + last
            out[v, CL - 2, :, lanes] = full[v, CL, :, lanes] + prior
            start.append((prior, last))

        def body(t, carried):
            i = CL - 3 - t
            following = []
            for v in range(NV):
                s = SETS[v]
                x1, x2 = carried[v]
                x = (0.5 * forced(v, i) - x2) * tail[s, i, :, lanes] - lead[s, i, :, lanes] * x1
                out[v, i, :, lanes] = full[v, i + 2, :, lanes] + x
                following.append((x, x1))
            return tuple(following)

        lax.fori_loop(0, CL - 2, body, tuple(start), unroll=2)

    eliminate(0)
    first_ends = trade(ends.at[0], ends_in.at[0], 0)
    eliminate(1)
    second_ends = trade(ends.at[1], ends_in.at[1], 1)
    settle(shared + first_ends)
    solve_interface(ends_in.at[0], corners_in, forces.at[0], 0)
    first_forces = trade(forces.at[0], forces_in.at[0], 2)
    settle(second_ends)
    solve_interface(ends_in.at[1], corners_in, forces.at[1], 1)
    second_forces = trade(forces.at[1], forces_in.at[1], 3)
    settle(first_forces)
    substitute(0)
    settle(second_forces)
    substitute(1)


def on_device(
    state, axial_speed, sound_speed, cross_speed, donor_base, donor_frac, fringe_cell, live_count
):
    sems = pltpu.SemaphoreType.DMA
    block = (NV, CL, CJ, NK)
    part = pltpu.VMEM((3, CL, CJ, NK), F32)
    edge = pltpu.VMEM((NV, 2, CL, NK), F32)
    split = pltpu.VMEM((2, NV, 2, CL, 128), F32)
    packs = pltpu.VMEM((NCROSS, 8, 128), F32)
    shares = pltpu.VMEM((2, NLINE, 24, 128), F32)
    result = pl.pallas_call(
        step_kernel,
        out_shape=jax.ShapeDtypeStruct(block, F32),
        in_specs=[HBM_SPEC] * 3 + [SMEM_SPEC] + [HBM_SPEC] * 4,
        out_specs=VMEM_SPEC,
        scratch_shapes=[
            pltpu.VMEM((NCROSS, CAP), jnp.int32),
            pltpu.VMEM((3, NCROSS, CAP), F32),
            pltpu.VMEM((NCROSS, CAP), jnp.int32),
            pltpu.VMEM((CL + 2, CJ, NK), F32),
            pltpu.VMEM((CL + 2, CJ, NK), F32),
            pltpu.VMEM((CL, CJ, NK), F32),
            pltpu.VMEM((NV, CL + 4, CJ, NK), F32),
            pltpu.VMEM((4, NV, NK, 256), BF16),
            pltpu.VMEM((2, 4, 256, CAP), BF16),
            packs,
            packs,
            pltpu.VMEM((2, CL, NK), F32),
            pltpu.VMEM((2, CL, NK), F32),
            pltpu.VMEM((4, CJ, NK), F32),
            pltpu.VMEM((2, NV, 2, CJ, NK), F32),
            pltpu.VMEM((2, NV, 2, CJ, NK), F32),
            pltpu.VMEM((3, NCROSS, CAP), jnp.int32),
            pltpu.VMEM((2, NV, 2, CL, NK), F32),
            edge,
            edge,
            split,
            split,
            pltpu.VMEM((2, 2, CL, 128), F32),
            pltpu.VMEM((NCROSS, 8, CAP), F32),
            pltpu.VMEM((3, NCROSS, 8, CAP), F32),
            part,
            part,
            part,
            part,
            part,
            pltpu.VMEM((33, CJ, 128), F32),
            pltpu.VMEM((CJ, 32, NK), F32),
            pltpu.VMEM((NLINE, 32, NK), F32),
            pltpu.VMEM((3, NK, NCROSS * CAP), BF16),
            pltpu.VMEM((3, NK, NCROSS * CAP), F8),
            pltpu.VMEM((NV * 128, NCROSS * CAP), BF16),
            pltpu.VMEM(((NV + 1) * 128, NCROSS * CAP), F8),
            pltpu.VMEM(block, F32),
            shares,
            shares,
            shares,
            shares,
            sems((7,)),
            sems,
            sems((15,)),
            sems((8,)),
            sems((8,)),
            sems((7,)),
            sems((7,)),
            sems,
            sems,
            sems((2,)),
            sems((2,)),
            sems((2,)),
            sems((2,)),
            sems((2,)),
            sems((2,)),
            sems((4, 7)),
            sems((4, 7)),
        ],
        compiler_params=pltpu.CompilerParams(collective_id=0, has_side_effects=True, vmem_limit_bytes=LIMIT),
        name="step",
    )(
        donor_base.reshape(NCROSS, CAP),
        donor_frac.reshape(3, NCROSS, CAP),
        fringe_cell.reshape(NCROSS, CAP),
        live_count.reshape(NCROSS),
        axial_speed,
        sound_speed,
        cross_speed,
        state,
    )
    return pl.pallas_call(
        deliver_kernel,
        out_shape=jax.ShapeDtypeStruct(block, F32),
        in_specs=[HBM_SPEC],
        out_specs=HBM_SPEC,
        scratch_shapes=[pltpu.VMEM(block, F32), sems((NV,)), sems((NV,))],
        compiler_params=pltpu.CompilerParams(vmem_limit_bytes=LIMIT),
        name="deliver",
    )(result)


def deliver_kernel(source, target, held, arrived, left):
    steps = []
    for v in range(NV):
        steps.append(
            (
                pltpu.make_async_copy(source.at[v], held.at[v], arrived.at[v]),
                pltpu.make_async_copy(held.at[v], target.at[v], left.at[v]),
            )
        )
        steps[v][0].start()
    for come, go in steps:
        come.wait()
        go.start()
    for _, go in steps:
        go.wait()


def solution(mesh):
    in_specs = (
        P(None, "line", "cross", None),
        P("line", "cross", None),
        P("line", "cross", None),
        P("line", "cross", None),
        P("line", "cross", None, None),
        P("line", "cross", None, None, None),
        P("line", "cross", None, None),
        P("line", "cross", None),
    )
    out_specs = P(None, "line", "cross", None)
    return jax.shard_map(
        on_device, mesh=mesh, in_specs=in_specs, out_specs=out_specs, check_vma=False
    )
```

```python
import jax
import jax.numpy as jnp
from jax import lax
from jax.experimental import pallas as pl
from jax.experimental.pallas import tpu as pltpu
from jax.sharding import PartitionSpec as P

MESH = pl.DeviceIdType.MESH
F32 = jnp.float32
BF16 = jnp.bfloat16
NV, CL, CJ, NK, CAP = 5, 64, 8, 256, 256
NLINE, NCROSS = 8, 16
SETS = (0, 1, 1, 1, 2)
SIGMA = (-1.0, 0.0, 1.0)
ONE, TWO, MID = -264.0, 2.0, 524.0
F8 = jnp.float8_e4m3fn
LIMIT = 56 * 1024 * 1024
TRANSPOSED = (((1,), (1,)), ((), ()))

VMEM_SPEC = pl.BlockSpec(memory_space=pltpu.VMEM)
SMEM_SPEC = pl.BlockSpec(memory_space=pltpu.SMEM)
HBM_SPEC = pl.BlockSpec(memory_space=pltpu.HBM)


def remote(src, dst, send, recv, device):
    copy = pltpu.make_async_remote_copy(
        src_ref=src, dst_ref=dst, send_sem=send, recv_sem=recv, device_id=device, device_id_type=MESH
    )
    copy.start()
    return copy


def around(axis):
    count = {"line": NLINE, "cross": NCROSS}[axis]
    me = lax.axis_index(axis)
    return me, [lax.rem(me + d, count) for d in range(1, count)]


def build_tables(full, tables):
    odd = lax.bitwise_and(lax.broadcasted_iota(jnp.int32, (CL // 2, CJ, NK), 1), 1) == 1

    @pl.loop(0, NV)
    def _(v):
        pairs = full[v, pl.ds(2, CL)].reshape(CL // 2, 2, CJ, NK)
        for a in range(2):
            high = pairs[:, a].astype(BF16).astype(F32)
            low = pairs[:, a] - high
            for b in range(2):
                if b == 0:
                    mixed = jnp.where(odd, pltpu.roll(low, 1, 1), high)
                else:
                    mixed = jnp.where(odd, high, pltpu.roll(low, CJ - 1, 1))
                tables[2 * a + b, v] = mixed.reshape(256, NK).T.astype(BF16)


def read_request(asked):
    def field(q):
        return jnp.concatenate([asked[2 * q : 2 * q + 1, :], asked[2 * q + 1 : 2 * q + 2, :]], 1)

    origin = field(0).astype(jnp.int32)
    row = lax.shift_right_logical(origin, 11)
    column = lax.bitwise_and(lax.shift_right_logical(origin, 8), 7)
    return row, column, lax.bitwise_and(origin, 255), field(1), field(2), field(3)


def build_hots(asked, hots, slot):
    row, column, _, _, _, _ = read_request(asked)
    place = lax.shift_right_logical(lax.broadcasted_iota(jnp.int32, (256, CAP), 0), 1)
    for a in range(2):
        for b in range(2):
            corner = lax.shift_right_logical(row + 1 - a, 1) * 4 + lax.shift_right_logical(column + 1 - b, 1)
            hots[slot, 2 * a + b] = jnp.where(place == corner, 1.0, 0.0).astype(BF16)


def donor_products(asked, tables, hots, slot):
    row, column, depth, fx, fy, fz = read_request(asked)
    even_row = lax.bitwise_and(row, 1) == 0
    even_column = lax.bitwise_and(column, 1) == 0
    gx, gy, gz = 1.0 - fx, 1.0 - fy, 1.0 - fz
    along_x = (jnp.where(even_row, gx, fx), jnp.where(even_row, fx, gx))
    along_y = (jnp.where(even_column, gy, fy), jnp.where(even_column, fy, gy))
    past = lax.broadcasted_iota(jnp.int32, (NK, CAP), 0) - depth
    along_z = jnp.where(past == 0, gz, jnp.where(past == 1, fz, 0.0))
    sums = [0.0] * NV
    for a in range(2):
        for b in range(2):
            weight = along_x[a] * along_y[b]
            rows = tables[2 * a + b].reshape(NV * NK, 256)
            mixed = jnp.dot(rows, hots[slot, 2 * a + b], preferred_element_type=F32)
            for v in range(NV):
                sums[v] += weight * jnp.sum(mixed[v * NK : (v + 1) * NK] * along_z, axis=0, keepdims=True)
    return jnp.concatenate(sums + [jnp.zeros((3, CAP), F32)], 0)


def build_depths(cells, m, wide, narrow):
    for p in range(NCROSS):
        depth = lax.bitwise_and(cells[m, p : p + 1, :], 255)
        hit = jnp.where(lax.broadcasted_iota(jnp.int32, (NK, CAP), 0) == depth, 1.0, 0.0)
        wide[:, p * CAP : (p + 1) * CAP] = hit.astype(BF16)
        narrow[:, p * CAP : (p + 1) * CAP] = hit.astype(F8)


def place_values(values, cells, m, rows, wide, narrow, high_part, low_part):
    count = rows.shape[0]
    peak = jnp.maximum(jnp.max(jnp.abs(values[m]), axis=(0, 1, 2), keepdims=True)[0], 1e-30)
    scale = 65536.0 / peak
    for p in range(NCROSS):
        lanes = slice(p * CAP, (p + 1) * CAP)
        hit = rows == lax.shift_right_arithmetic(cells[m, p : p + 1, :], 8)
        picked = jnp.where(hit, 1.0, 0.0).astype(BF16)
        for v in range(NV):
            here = values[m, p, v : v + 1, :]
            high = here.astype(BF16)
            low = ((here - high.astype(F32)) * scale).astype(BF16)
            high_part[v * count : (v + 1) * count, lanes] = picked * high
            low_part[v * count : (v + 1) * count, lanes] = (picked * low).astype(F8)
        low_part[NV * count : (NV + 1) * count, lanes] = picked.astype(F8)
    high = lax.dot_general(high_part[0 : NV * count], wide[...], TRANSPOSED, preferred_element_type=F32)
    low = lax.dot_general(low_part[0 : (NV + 1) * count], narrow[...], TRANSPOSED, preferred_element_type=F32)
    unscale = peak * (1.0 / 65536.0)
    fresh = [
        high[v * count : (v + 1) * count] + low[v * count : (v + 1) * count] * unscale for v in range(NV)
    ]
    return low[NV * count :] > 0.5, fresh


def factor_rows(axial, sound, lead, tail, first, second, inverse, carry, start, base, lanes):
    state = [[jnp.where(start, 0.0, carry[11 * s + n]) for n in range(11)] for s in range(3)]
    for k in range(8):
        i = base + k
        speed, wave = axial[i + 1, :, lanes], sound[i + 1, :, lanes]
        rho = jnp.abs(speed) + wave
        for s in range(3):
            e1, p1, q1, q2, a1, a2, b1, b2, aa, ab, bb = state[s]
            r = 1.0 / (rho + 0.5 * jnp.abs(speed + SIGMA[s] * wave))
            inv = 1.0 / ((MID + r) - TWO * q2 - e1 * p1)
            e = ONE - TWO * p1
            p = e * inv
            q = TWO * inv
            a = 0.0 - p1 * a1 - q2 * a2
            b = 0.0 - p1 * b1 - q2 * b2
            if k == 0:
                a = jnp.where(start, 1.0, a)
            if k == 1:
                b = jnp.where(start, 1.0, b)
            ai, bi = a * inv, b * inv
            lead[s, i, :, lanes], tail[s, i, :, lanes] = p, q
            first[s, i, :, lanes], second[s, i, :, lanes], inverse[s, i, :, lanes] = a, b, r
            state[s] = [e, p, q, q1, a, a1, b, b1, aa + ai * a, ab + ai * b, bb + bi * b]
    for s in range(3):
        for n in range(11):
            carry[11 * s + n] = state[s][n]


def inverse_corners(lead, carry, corners, half):
    lanes = pl.ds(half * 128, 128)
    for s in range(3):
        _, _, q1, q2, a1, a2, b1, b2, aa, ab, bb = [carry[11 * s + n] for n in range(11)]
        inv1, inv2, p2 = 0.5 * q1, 0.5 * q2, lead[s, CL - 2, :, lanes]
        entries = (
            aa,
            ab,
            bb,
            a2 * inv2 - a1 * p2 * inv1,
            a1 * inv1,
            b2 * inv2 - b1 * p2 * inv1,
            b1 * inv1,
            inv2 + p2 * p2 * inv1,
            -p2 * inv1,
            inv1,
        )
        for m, entry in enumerate(entries):
            corners[:, 3 * m + s, lanes] = entry


def times(m, n):
    a, b, c, d = m
    e, f, g, h = n
    return (a * e + b * g, a * f + b * h, c * e + d * g, c * f + d * h)


def apply(m, x):
    return (m[0] * x[0] + m[1] * x[1], m[2] * x[0] + m[3] * x[1])


def right_upper(m):
    return (TWO * m[0], ONE * m[0] + TWO * m[1], TWO * m[2], ONE * m[2] + TWO * m[3])


def right_lower(m):
    return (TWO * m[0] + ONE * m[1], TWO * m[1], TWO * m[2] + ONE * m[3], TWO * m[3])


def plus(m, n):
    return tuple(a + b for a, b in zip(m, n))


def minus(m, n):
    return tuple(a - b for a, b in zip(m, n))


def solve_interface(ends, corners, forces, half):
    lanes = slice(half * 128, half * 128 + 128)
    variable = lax.broadcasted_iota(jnp.int32, (NV, 128), 0)

    def corner(l, m):
        rows = [corners[l, 3 * m + s : 3 * m + s + 1, lanes] for s in range(3)]
        return jnp.where(variable == 0, rows[0], jnp.where(variable == 4, rows[2], rows[1]))

    steps = []
    p = m = None
    for l in range(NLINE):
        c = [corner(l, k) for k in range(10)]
        heads = (c[0], c[1], c[1], c[2])
        cross = (c[3], c[4], c[5], c[6])
        back = (c[3], c[5], c[4], c[6])
        tails = (c[7], c[8], c[8], c[9])
        ya = (ends[l, 0:5, :], ends[l, 5:10, :])
        yb = (ends[l, 10:15, :], ends[l, 15:20, :])
        if l == 0:
            inner, reach = ya, right_lower(cross)
            p, m = yb, right_lower(tails)
        else:
            heads_u, back_u = right_upper(heads), right_upper(back)
            t = times(heads_u, m)
            g = (1.0 - t[0], -t[1], -t[2], 1.0 - t[3])
            scale = 1.0 / (g[0] * g[3] - g[1] * g[2])
            g = (g[3] * scale, -g[1] * scale, -g[2] * scale, g[0] * scale)
            inner = apply(g, minus(ya, apply(heads_u, p)))
            reach = right_lower(times(g, cross))
            back_um = times(back_u, m)
            p = plus(minus(yb, apply(back_u, p)), apply(back_um, inner))
            m = plus(right_lower(tails), times(back_um, reach))
        steps.append((inner, reach, p, m))
    a = None
    for l in reversed(range(NLINE)):
        inner, reach, _, _ = steps[l]
        zero = ends[0, 0:5, :] * 0.0
        if l == NLINE - 1:
            beta = (zero, zero)
            a = inner
        else:
            beta = (TWO * a[0], ONE * a[0] + TWO * a[1])
            a = minus(inner, apply(reach, a))
        if l == 0:
            alpha = (zero, zero)
        else:
            _, _, p, m = steps[l - 1]
            b = minus(p, apply(m, a))
            alpha = (TWO * b[0] + ONE * b[1], TWO * b[1])
        for m, value in enumerate(alpha + beta):
            forces[l, 5 * m : 5 * m + 5, :] = value


def step_kernel(
    base, frac, cell, live, axial_hbm, sound_hbm, crossing_hbm, state, out,
    base_here, frac_here, cell_here, axial, sound, crossing, full, tables, hots, packed, inbox, cross_out, cross_in, line_in, rows_out, rows_in,
    cells, edges, before_raw, after_raw, before, after, crosses_by, values, lists,
    lead, tail, first, second, inverse, carry, corners, corners_in, wide, narrow, high_part, low_part,
    eliminated, ends, ends_in, forces, forces_in,
    load, ask_send, ask_recv, fixed_send, fixed_recv, corner_send, corner_recv, value_send, value_recv, pass_send, pass_recv,
    row_send, row_recv, edge_send, edge_recv, trade_send, trade_recv,
):
    me, peers = around("cross")
    row, others = around("line")
    down, up = others[0], others[-1]
    rightward, leftward = peers[0], peers[-1]

    loads = []
    for source, target in (
        (base, base_here),
        (frac, frac_here),
        (cell, cell_here),
        (state, full.at[:, pl.ds(2, CL)]),
        (axial_hbm, axial.at[pl.ds(1, CL)]),
        (sound_hbm, sound.at[pl.ds(1, CL)]),
        (crossing_hbm, crossing),
    ):
        loads.append(pltpu.make_async_copy(source, target, load.at[len(loads)]))
        loads[-1].start()
    barrier = pltpu.get_barrier_semaphore()
    partners = [(row, p) for p in peers] + [(r, me) for r in others]
    for device in partners:
        pl.semaphore_signal(barrier, inc=1, device_id=device, device_id_type=MESH)

    for copy in loads[:3]:
        copy.wait()
    for half in range(2):
        lanes = pl.ds(half * 128, 128)
        packed[:, half, :] = base_here[:, lanes].astype(F32)
        for q in range(3):
            packed[:, 2 * q + 2 + half, :] = frac_here[q, :, lanes]
    inbox[me] = packed[me]
    slot = lax.broadcasted_iota(jnp.int32, (1, CAP), 1)
    for p in range(NCROSS):
        cells[0, p : p + 1, :] = jnp.where(slot < live[p], cell_here[p : p + 1, :], -1)

    for copy in loads[3:]:
        copy.wait()
    cross_out[0] = crossing[:, 0, :]
    cross_out[1] = crossing[:, CJ - 1, :]

    @pl.loop(0, NV)
    def _(v):
        for j in range(2):
            edges[0, v, j] = full[v, pl.ds(2, CL), j, :]
            edges[1, v, j] = full[v, pl.ds(2, CL), CJ - 2 + j, :]

    pl.semaphore_wait(barrier, len(partners))
    for d, p in reversed(list(enumerate(peers))):
        remote(packed.at[p], inbox.at[me], ask_send, ask_recv.at[d], (row, p))
    fixed = []

    def fix(source, target, device):
        m = len(fixed)
        fixed.append(remote(source, target, fixed_send.at[m], fixed_recv.at[m], device))

    fix(cells.at[0], cells.at[2], (row, leftward))
    fix(cells.at[0], cells.at[1], (row, rightward))
    fix(axial.at[1], line_in.at[2], (up, me))
    fix(sound.at[1], line_in.at[3], (up, me))
    fix(axial.at[CL], line_in.at[0], (down, me))
    fix(sound.at[CL], line_in.at[1], (down, me))
    fix(cross_out.at[0], cross_in.at[1], (row, leftward))
    fix(cross_out.at[1], cross_in.at[0], (row, rightward))

    def send_edge(side, v):
        target, device = ((after_raw, (row, leftward)), (before_raw, (row, rightward)))[side]
        remote(edges.at[side, v], target.at[v], edge_send.at[side], edge_recv.at[side], device)

    build_tables(full, tables)
    build_depths(cells, 0, wide.at[0], narrow.at[0])
    build_hots(inbox[me], hots, 0)
    corners[...] = jnp.zeros(corners.shape, F32)

    @pl.loop(0, NCROSS // 2)
    def _(h):
        for k in range(2):
            d = 2 * h + k
            p = lax.rem(me + d, NCROSS)
            ahead = lax.rem(me + d + 1, NCROSS)

            @pl.when(d < 15)
            def _():
                pltpu.make_async_remote_copy(
                    src_ref=packed.at[ahead], dst_ref=inbox.at[ahead], send_sem=ask_send,
                    recv_sem=ask_recv.at[14 - d], device_id=(row, ahead), device_id_type=MESH,
                ).wait_recv()

            build_hots(inbox[ahead], hots, 1 - k)
            answer = donor_products(inbox[p], tables, hots, k)
            values[p] = answer

            @pl.when(h < NV)
            def _():
                send_edge(k, h)

            lanes = pl.ds(pl.multiple_of((h // 4) * 128, 128), 128)
            start = d % 8 == 0
            @pl.when(d == 0)
            def _():
                lists[0, me] = answer

            @pl.when(d > 0)
            def _():
                remote(values.at[p], lists.at[0, me], value_send, value_recv, (row, p))

    for half in range(2):

        @pl.loop(0, 8)
        def _(block):
            lanes = pl.ds(half * 128, 128)
            factor_rows(axial, sound, lead, tail, first, second, inverse, carry, block == 0, block * 8, lanes)

        inverse_corners(lead, carry, corners, half)
    shared = [
        remote(corners.at[r], corners_in.at[row], corner_send.at[d], corner_recv.at[d], (r, me))
        for d, r in enumerate(others)
    ]
    corners_in[row] = corners[row]
    for copy in fixed:
        copy.wait()
    axial[0], sound[0], axial[CL + 1], sound[CL + 1] = line_in[0], line_in[1], line_in[2], line_in[3]
    for half in range(2):
        crosses_by[half] = cross_in[:, :, pl.ds(half * 128, 128)]
    for m in range(1, 3):
        build_depths(cells, m, wide.at[m], narrow.at[m])

    most = pl.ds(0, 15)
    pltpu.make_async_remote_copy(
        src_ref=packed.at[most], dst_ref=inbox.at[most], send_sem=ask_send, recv_sem=ask_recv.at[0],
        device_id=(row, rightward), device_id_type=MESH,
    ).wait_send()
    pltpu.make_async_remote_copy(
        src_ref=values.at[most], dst_ref=lists.at[0, most], send_sem=value_send, recv_sem=value_recv,
        device_id=(row, rightward), device_id_type=MESH,
    ).wait()
    passed = [
        remote(lists.at[0], lists.at[1], pass_send.at[0], pass_recv.at[0], (row, rightward)),
        remote(lists.at[0], lists.at[2], pass_send.at[1], pass_recv.at[1], (row, leftward)),
    ]

    def inside(flag, value):
        return jnp.where(flag, value, 0.0)

    @pl.loop(0, 4)
    def _(n):
        t = (3 * n) % 4
        rows = lax.broadcasted_iota(jnp.int32, (128, CAP), 0) + t * 128
        taken, fresh = place_values(lists, cells, 0, rows, wide.at[0], narrow.at[0], high_part, low_part)
        span = pl.ds(2 + t * 16, 16)
        for v in range(NV):
            full[v, span] = jnp.where(taken, fresh[v], full[v, span].reshape(128, NK)).reshape(16, CJ, NK)

        @pl.when(n == 1)
        def _():
            rows_out[0] = full[:, pl.ds(2, 2)]
            rows_out[1] = full[:, pl.ds(CL, 2)]
            remote(rows_out.at[0], rows_in.at[1], row_send.at[0], row_recv.at[0], (up, me))
            remote(rows_out.at[1], rows_in.at[0], row_send.at[1], row_recv.at[1], (down, me))

    for copy in passed:
        copy.wait()
    for side, raw in enumerate((after_raw, before_raw)):
        pltpu.make_async_remote_copy(
            src_ref=edges.at[side], dst_ref=raw, send_sem=edge_send.at[side], recv_sem=edge_recv.at[side],
            device_id=(row, (leftward, rightward)[side]), device_id_type=MESH,
        ).wait()
    for m, column, raw, target, flag in (
        (1, CJ - 2, before_raw, before, me > 0),
        (2, 0, after_raw, after, me < NCROSS - 1),
    ):
        order = lax.broadcasted_iota(jnp.int32, (128, CAP), 0)
        rows = lax.bitwise_and(order, 63) * CJ + column + lax.shift_right_logical(order, 6)
        taken, fresh = place_values(lists, cells, m, rows, wide.at[m], narrow.at[m], high_part, low_part)
        for v in range(NV):
            now = inside(flag, jnp.where(taken, fresh[v], raw[v].reshape(128, NK)))
            for j in range(2):
                for half in range(2):
                    target[half, v, j] = now[j * CL : (j + 1) * CL, half * 128 : half * 128 + 128]
    for m, device in enumerate((up, down)):
        pltpu.make_async_remote_copy(
            src_ref=rows_out.at[m], dst_ref=rows_in.at[1 - m], send_sem=row_send.at[m], recv_sem=row_recv.at[m],
            device_id=(device, me), device_id_type=MESH,
        ).wait()
    full[:, pl.ds(0, 2)] = inside(row > 0, rows_in[0])
    full[:, pl.ds(CL + 2, 2)] = inside(row < NLINE - 1, rows_in[1])

    ends[...] = jnp.zeros(ends.shape, F32)
    column = lax.broadcasted_iota(jnp.int32, (CJ, 128), 0)

    def eliminate(half):
        lanes = pl.ds(half * 128, 128)
        zero = sound[1, :, lanes] * 0.0

        def body(i, carried):
            speed, wave, crosses = axial[i + 1, :, lanes], sound[i + 1, :, lanes], crossing[i, :, lanes]
            rho = jnp.abs(speed) + wave
            speed_up, wave_up = axial[i, :, lanes], sound[i, :, lanes]
            speed_down, wave_down = axial[i + 2, :, lanes], sound[i + 2, :, lanes]
            here = pl.ds(i, 1)
            cross_left = jnp.where(column == 0, crosses_by[half, 0, here, :], pltpu.roll(crosses, 1, 0))
            cross_right = jnp.where(column == CJ - 1, crosses_by[half, 1, here, :], pltpu.roll(crosses, CJ - 1, 0))
            by_left, by_right = rho + 4.0 * cross_left, rho - 4.0 * cross_right
            rho32, by_two, by_here = 32.0 * rho, 8.0 * rho, 49.5 * rho
            by_above = [rho32 + 4.0 * (speed_up + SIGMA[s] * wave_up) for s in range(3)]
            by_below = [rho32 - 4.0 * (speed_down + SIGMA[s] * wave_down) for s in range(3)]
            following = []
            for v in range(NV):
                s = SETS[v]
                y1, y2, low, high = carried[v]
                q = full[v, i + 2, :, lanes]
                l2, l1 = before[half, v, 0, here, :], before[half, v, 1, here, :]
                r1, r2 = after[half, v, 0, here, :], after[half, v, 1, here, :]
                left1 = jnp.where(column == 0, l1, pltpu.roll(q, 1, 0))
                left2 = jnp.where(column == 0, l2, jnp.where(column == 1, l1, pltpu.roll(q, 2, 0)))
                right1 = jnp.where(column == CJ - 1, r1, pltpu.roll(q, CJ - 1, 0))
                right2 = jnp.where(column == CJ - 1, r2, jnp.where(column == CJ - 2, r1, pltpu.roll(q, CJ - 2, 0)))
                two = (full[v, i, :, lanes] + full[v, i + 4, :, lanes]) + 0.03125 * (left2 + right2)
                source = (
                    (by_above[s] * full[v, i + 1, :, lanes] + by_below[s] * full[v, i + 3, :, lanes])
                    + (by_left * left1 + by_right * right1)
                    - (by_two * two + by_here * q)
                )
                p1 = lead[s, jnp.maximum(i - 1, 0), :, lanes]
                q2 = tail[s, jnp.maximum(i - 2, 0), :, lanes]
                y = (source * inverse[s, i, :, lanes] - q2 * y2) - p1 * y1
                eliminated[v, i, :, lanes] = y
                t = y * (0.5 * tail[s, i, :, lanes])
                following.append((y, y1, low + first[s, i, :, lanes] * t, high + second[s, i, :, lanes] * t))
            return tuple(following)

        done = lax.fori_loop(0, CL, body, (((zero,) * 4),) * NV, unroll=4)
        for v in range(NV):
            s = SETS[v]
            y1, y2, low, high = done[v]
            last = 0.5 * tail[s, CL - 1, :, lanes] * y1
            ends[half, :, v, :] = low
            ends[half, :, 5 + v, :] = high
            ends[half, :, 10 + v, :] = 0.5 * tail[s, CL - 2, :, lanes] * y2 - lead[s, CL - 2, :, lanes] * last
            ends[half, :, 15 + v, :] = last

    def trade(source, target, m):
        copies = [
            remote(source.at[r], target.at[row], trade_send.at[m, d], trade_recv.at[m, d], (r, me))
            for d, r in enumerate(others)
        ]
        target[row] = source[row]
        return copies

    def settle(copies):
        for copy in copies:
            copy.wait()

    def substitute(half):
        lanes = pl.ds(half * 128, 128)

        def forced(v, i):
            s = SETS[v]
            alpha0, alpha1 = forces_in[half, :, v, :], forces_in[half, :, 5 + v, :]
            return eliminated[v, i, :, lanes] - first[s, i, :, lanes] * alpha0 - second[s, i, :, lanes] * alpha1

        start = []
        for v in range(NV):
            s = SETS[v]
            beta0, beta1 = forces_in[half, :, 10 + v, :], forces_in[half, :, 15 + v, :]
            p2 = lead[s, CL - 2, :, lanes]
            last = (forced(v, CL - 1) - beta1 + p2 * beta0) * (0.5 * tail[s, CL - 1, :, lanes])
            prior = (forced(v, CL - 2) - beta0) * (0.5 * tail[s, CL - 2, :, lanes]) - p2 * last
            out[v, CL - 1, :, lanes] = full[v, CL + 1, :, lanes] + last
            out[v, CL - 2, :, lanes] = full[v, CL, :, lanes] + prior
            start.append((prior, last))

        def body(t, carried):
            i = CL - 3 - t
            following = []
            for v in range(NV):
                s = SETS[v]
                x1, x2 = carried[v]
                x = (0.5 * forced(v, i) - x2) * tail[s, i, :, lanes] - lead[s, i, :, lanes] * x1
                out[v, i, :, lanes] = full[v, i + 2, :, lanes] + x
                following.append((x, x1))
            return tuple(following)

        lax.fori_loop(0, CL - 2, body, tuple(start), unroll=4)

    eliminate(0)
    first_ends = trade(ends.at[0], ends_in.at[0], 0)
    eliminate(1)
    second_ends = trade(ends.at[1], ends_in.at[1], 1)
    settle(shared + first_ends)
    solve_interface(ends_in.at[0], corners_in, forces.at[0], 0)
    first_forces = trade(forces.at[0], forces_in.at[0], 2)
    settle(second_ends)
    solve_interface(ends_in.at[1], corners_in, forces.at[1], 1)
    second_forces = trade(forces.at[1], forces_in.at[1], 3)
    settle(first_forces)
    substitute(0)
    settle(second_forces)
    substitute(1)


def on_device(
    state, axial_speed, sound_speed, cross_speed, donor_base, donor_frac, fringe_cell, live_count
):
    sems = pltpu.SemaphoreType.DMA
    block = (NV, CL, CJ, NK)
    part = pltpu.VMEM((3, CL, CJ, NK), F32)
    edge = pltpu.VMEM((NV, 2, CL, NK), F32)
    split = pltpu.VMEM((2, NV, 2, CL, 128), F32)
    packs = pltpu.VMEM((NCROSS, 8, 128), F32)
    shares = pltpu.VMEM((2, NLINE, 24, 128), F32)
    result = pl.pallas_call(
        step_kernel,
        out_shape=jax.ShapeDtypeStruct(block, F32),
        in_specs=[HBM_SPEC] * 3 + [SMEM_SPEC] + [HBM_SPEC] * 4,
        out_specs=VMEM_SPEC,
        scratch_shapes=[
            pltpu.VMEM((NCROSS, CAP), jnp.int32),
            pltpu.VMEM((3, NCROSS, CAP), F32),
            pltpu.VMEM((NCROSS, CAP), jnp.int32),
            pltpu.VMEM((CL + 2, CJ, NK), F32),
            pltpu.VMEM((CL + 2, CJ, NK), F32),
            pltpu.VMEM((CL, CJ, NK), F32),
            pltpu.VMEM((NV, CL + 4, CJ, NK), F32),
            pltpu.VMEM((4, NV, NK, 256), BF16),
            pltpu.VMEM((2, 4, 256, CAP), BF16),
            packs,
            packs,
            pltpu.VMEM((2, CL, NK), F32),
            pltpu.VMEM((2, CL, NK), F32),
            pltpu.VMEM((4, CJ, NK), F32),
            pltpu.VMEM((2, NV, 2, CJ, NK), F32),
            pltpu.VMEM((2, NV, 2, CJ, NK), F32),
            pltpu.VMEM((3, NCROSS, CAP), jnp.int32),
            pltpu.VMEM((2, NV, 2, CL, NK), F32),
            edge,
            edge,
            split,
            split,
            pltpu.VMEM((2, 2, CL, 128), F32),
            pltpu.VMEM((NCROSS, 8, CAP), F32),
            pltpu.VMEM((3, NCROSS, 8, CAP), F32),
            part,
            part,
            part,
            part,
            part,
            pltpu.VMEM((33, CJ, 128), F32),
            pltpu.VMEM((CJ, 32, NK), F32),
            pltpu.VMEM((NLINE, 32, NK), F32),
            pltpu.VMEM((3, NK, NCROSS * CAP), BF16),
            pltpu.VMEM((3, NK, NCROSS * CAP), F8),
            pltpu.VMEM((NV * 128, NCROSS * CAP), BF16),
            pltpu.VMEM(((NV + 1) * 128, NCROSS * CAP), F8),
            pltpu.VMEM(block, F32),
            shares,
            shares,
            shares,
            shares,
            sems((7,)),
            sems,
            sems((15,)),
            sems((8,)),
            sems((8,)),
            sems((7,)),
            sems((7,)),
            sems,
            sems,
            sems((2,)),
            sems((2,)),
            sems((2,)),
            sems((2,)),
            sems((2,)),
            sems((2,)),
            sems((4, 7)),
            sems((4, 7)),
        ],
        compiler_params=pltpu.CompilerParams(collective_id=0, has_side_effects=True, vmem_limit_bytes=LIMIT),
        name="step",
    )(
        donor_base.reshape(NCROSS, CAP),
        donor_frac.reshape(3, NCROSS, CAP),
        fringe_cell.reshape(NCROSS, CAP),
        live_count.reshape(NCROSS),
        axial_speed,
        sound_speed,
        cross_speed,
        state,
    )
    return pl.pallas_call(
        deliver_kernel,
        out_shape=jax.ShapeDtypeStruct(block, F32),
        in_specs=[HBM_SPEC],
        out_specs=HBM_SPEC,
        scratch_shapes=[pltpu.VMEM(block, F32), sems((NV,)), sems((NV,))],
        compiler_params=pltpu.CompilerParams(vmem_limit_bytes=LIMIT),
        name="deliver",
    )(result)


def deliver_kernel(source, target, held, arrived, left):
    steps = []
    for v in range(NV):
        steps.append(
            (
                pltpu.make_async_copy(source.at[v], held.at[v], arrived.at[v]),
                pltpu.make_async_copy(held.at[v], target.at[v], left.at[v]),
            )
        )
        steps[v][0].start()
    for come, go in steps:
        come.wait()
        go.start()
    for _, go in steps:
        go.wait()


def solution(mesh):
    in_specs = (
        P(None, "line", "cross", None),
        P("line", "cross", None),
        P("line", "cross", None),
        P("line", "cross", None),
        P("line", "cross", None, None),
        P("line", "cross", None, None, None),
        P("line", "cross", None, None),
        P("line", "cross", None),
    )
    out_specs = P(None, "line", "cross", None)
    return jax.shard_map(
        on_device, mesh=mesh, in_specs=in_specs, out_specs=out_specs, check_vma=False
    )
```
